32 devices in a mesh: row: 4 (over y, x), col: 8 (over z, core).
Axes of the slice: x: 2, y: 2, z: 4, core: 2. Of those that a mesh axis runs over, the one named last changes fastest.
Arguments:
- density: float32 [2560, 2560], P('row', 'col'), as said below
- pattern: int32 [40, 40], P('row', 'col'), may hold values from 0 to 1, as said below
- weights: float32 [2560], P('row'), may hold values from 0.5 to 5
Outputs:
- purified: float32 [2560, 2560], P('row', 'col')
- checks: float32 [2, 2560], P(None, 'col')
The draws below stay inside these ranges and needn't reach their ends.
Inputs may be any that keep to these rules, and one draw needn't show every extreme that they name: pattern is symmetric, and every block with |a - b| <= 2 is nonzero; the number of nonzero blocks differs strongly between block rows. density is symmetric and zero outside the blocks that pattern marks.
All inputs are finite; a program needn't handle non-finite values.
Results may differ from the reference program's by a relative error of at most 0.00012.
Values sent between devices are 32-bit elements; how exact they have to be, the bound alone decides.
No kernel may reach another device: no remote copies, remote signals or barrier semaphores. Data moves between devices by JAX's collectives and lax.ppermute only.
A program may use at most 64 MiB of HBM per device.

```python
import math
import jax
import jax.numpy as jnp
from jax import lax

BLK = 64
ITERS = 1
NB = 40
N = 2560


def pattern_helper(key):
    base = jax.random.fold_in(key, 11)
    first_key, second_key = jax.random.split(base)
    limits = jax.random.randint(first_key, (NB,), 5, 45)
    rolled = jax.random.randint(second_key, (NB, NB), 0, 100)
    rolled = jnp.minimum(rolled, rolled.T)
    bound = jnp.minimum(limits[:, None], limits[None, :])
    index = jnp.arange(NB)
    banded = jnp.abs(index[:, None] - index[None, :]) <= 2
    return jnp.where(banded | (rolled < bound), 1, 0).astype(jnp.int32)


def draw_pattern(key, part):
    return pattern_helper(key)


def draw_density(key, part):
    blocks = pattern_helper(key)
    block_mask = jnp.repeat(jnp.repeat(blocks.astype(jnp.float32), BLK, axis=0), BLK, axis=1)
    noise_key = jax.random.fold_in(key, 23)
    raw = jax.random.normal(noise_key, (N, N), jnp.float32)
    sym = (raw + raw.T) * math.sqrt(0.5)
    sigma = 0.22 / math.sqrt(BLK * NB * 0.35)
    ident = jnp.eye(N, dtype=jnp.float32)
    return (block_mask * (0.5 * ident + sigma * sym)).astype(jnp.float32)


def block_scale(key, dims, pieces, smallest, high):
    gain, own = 1.0, jax.random.fold_in(key, 6)
    for position, shards_of in pieces:
        steps = jnp.exp(jax.random.uniform(jax.random.fold_in(own, position), (shards_of,), jnp.float32, smallest / len(pieces), high / len(pieces)))
        gain = gain * jnp.repeat(steps, dims[position] // shards_of).reshape([-1 if axis == position else 1 for axis in range(len(dims))])
    return gain


def setup_inputs(seed: int = 0) -> dict:
    key_of = jax.random.split(jax.random.key(seed), 4)
    density = draw_density(jax.random.fold_in(key_of[3], 71), 0)
    pattern = draw_pattern(jax.random.fold_in(key_of[3], 71), 0)
    weights = jnp.clip(jnp.exp(math.log(5.0) - 2.3025851 * jax.random.uniform(key_of[2], (N,), jnp.float32) ** block_scale(key_of[2], (N,), ((0, 4),), -0.2, 0.2)), 0.5, 5.0)
    return {"density": density, "pattern": pattern, "weights": weights}


def expand_mask(pattern):
    return jnp.repeat(jnp.repeat(pattern.astype(jnp.float32), BLK, axis=0), BLK, axis=1)


def full_dot(first, second):
    return jnp.dot(first, second, precision=lax.Precision.HIGHEST, preferred_element_type=jnp.float32)


def reference(density, pattern, weights):
    block_mask = expand_mask(pattern)
    current = density
    weight_row = weights[None, :]
    checks = []
    for iteration in range(ITERS):
        checks.append(full_dot(full_dot(weight_row, current), current))
        square = block_mask * full_dot(current, current)
        checks.append(full_dot(full_dot(weight_row, square), current))
        cube_term = block_mask * full_dot(square, current)
        current = 3.0 * square - 2.0 * cube_term
    return current, jnp.concatenate(checks, axis=0)
```

```python
import jax
import jax.numpy as jnp
from jax import lax
from jax.sharding import PartitionSpec as P

BLK = 64


def dot(first, second, contract=((1,), (0,))):
    return lax.dot_general(
        first, second, (contract, ((), ())), precision=lax.Precision.HIGH, preferred_element_type=jnp.float32
    )


def expand_mask(pattern):
    return jnp.repeat(jnp.repeat(pattern.astype(jnp.float32), BLK, axis=0), BLK, axis=1)


def make_body(panels, columns):
    assert columns == 2 * panels and panels & (panels - 1) == 0

    def flat(r, z, core):
        return r * columns + 2 * z + core

    def send(value, target):
        pairs = []
        for r in range(panels):
            for z in range(panels):
                to = target(r, z)
                if to is not None:
                    pairs += [(flat(r, z, core), flat(*to, core)) for core in (0, 1)]
        return lax.ppermute(value, ("row", "col"), pairs)

    def swap_core(value):
        return lax.ppermute(value, "col", [(c, c ^ 1) for c in range(columns)])

    def ring(step):
        return lambda r, z: (r, (z + step) % panels)

    def others_ring(step):
        def target(r, z):
            if z == r:
                return None
            line = [q for q in range(panels) if q != r]
            return (r, line[(line.index(z) + step) % len(line)])

        return target

    def across(m):
        return lambda r, z: (r ^ m, z)

    def to_diagonal(m):
        return lambda r, z: (r ^ m, z) if r ^ m == z else None

    def row_sum(value):
        m = 1
        while m < panels:
            value = value + send(value, across(m))
            m *= 2
        return value

    def gather_ring(value, ring_of, count):
        got = {0: value}
        for j in range(1, count // 2 + 1):
            got[j] = send(got[j - 1], ring_of(1))
        for j in range(count - 1, count // 2, -1):
            got[j] = send(got[(j + 1) % count], ring_of(-1))
        return got

    def body(density, pattern, weights):
        r = lax.axis_index("row")
        c = lax.axis_index("col")
        z, core = c // 2, c % 2
        half = density.shape[1]
        block_mask = expand_mask(pattern)
        line_pattern = lax.all_gather(pattern, "col", axis=0)
        diagonal_mask = expand_mask(lax.dynamic_index_in_dim(line_pattern, 2 * r + core, 0, keepdims=False))

        def own_rows(value):
            mine = lax.dynamic_slice_in_dim(value, core * half, half, 0)
            given = lax.dynamic_slice_in_dim(value, (1 - core) * half, half, 0)
            return mine, swap_core(given)

        def finish(kept_and_given):
            return kept_and_given[:, :half] + swap_core(kept_and_given[:, half:])

        left = gather_ring(density, ring, panels)
        own = jnp.concatenate(own_rows(density), axis=1)
        right = jnp.stack([own] + [send(own, across(m)) for m in range(1, panels)])

        def right_of(k):
            return lax.dynamic_index_in_dim(right, r ^ k, 0, keepdims=False)

        product = sum(dot(left[j], right_of((z - j) % panels)) for j in (0, 1, 3, 2) + tuple(range(4, panels)))
        product = finish(product)
        square = block_mask * product

        weight_row = weights[None, :]
        sums = row_sum(jnp.sum(jnp.stack([product, square]) * weights[None, :, None], axis=1))
        first_check, column_sums = sums[:1], sums[1]
        all_sums = lax.all_gather(column_sums, "col", axis=0).reshape(panels, 2, half)
        all_sums = lax.dynamic_index_in_dim(all_sums, core, 1, keepdims=False)
        ordered = jnp.take(all_sums, r ^ jnp.arange(panels), axis=0)
        second_partial = jnp.sum(right * ordered[:, :, None], axis=(0, 1))[None, :]
        second_check = finish(second_partial)

        others = gather_ring(square, others_ring, panels - 1)
        mine, theirs = own_rows(square)
        rows = jnp.where(core == 0, jnp.concatenate([mine, theirs], axis=1), jnp.concatenate([theirs, mine], axis=1))
        down = [send(rows, to_diagonal(m)) for m in range(1, panels)]

        def own_part(value, which):
            return lax.dynamic_slice_in_dim(value, which * half, half, 0)

        def diagonal(which):
            return sum(dot(left[j], own_part(left[j], which), ((1,), (1,))) for j in range(panels))

        diagonal_square = diagonal_mask * (diagonal(core) + swap_core(diagonal(1 - core)))

        place = z - (z > r).astype(z.dtype)

        def on_diagonal():
            return sum(dot(down[m - 1], right[m], ((0,), (0,))) for m in range(1, panels))

        def off_diagonal():
            total = dot(diagonal_square, right_of(r))
            for j in range(1, panels - 1):
                q = (place - j) % (panels - 1)
                total = total + dot(others[j], right_of(q + (q >= r).astype(q.dtype)))
            return total

        cube = dot(square, right_of(z)) + lax.cond(z == r, on_diagonal, off_diagonal)
        cube_term = block_mask * finish(cube)
        return 3.0 * square - 2.0 * cube_term, jnp.concatenate([first_check, second_check], axis=0)

    return body


def solution(mesh):
    in_specs = (P("row", "col"), P("row", "col"), P("row"))
    out_specs = (P("row", "col"), P(None, "col"))
    body = make_body(mesh.shape["row"], mesh.shape["col"])
    return jax.shard_map(body, mesh=mesh, in_specs=in_specs, out_specs=out_specs, check_vma=False)
```

```python
import functools

import jax
import jax.numpy as jnp
from jax import lax
from jax.experimental import pallas as pl
from jax.experimental.pallas import tpu as pltpu
from jax.sharding import PartitionSpec as P

BLK = 64
ROW_BY_COLUMN = ((1,), (0,))
ROW_BY_ROW = ((1,), (1,))


def expand_mask(pattern):
    return jnp.repeat(jnp.repeat(pattern.astype(jnp.float32), BLK, axis=0), BLK, axis=1)


def split(value):
    high = value.astype(jnp.bfloat16)
    return high, (value - high.astype(jnp.float32)).astype(jnp.bfloat16)


def dot(first, second, contract=ROW_BY_COLUMN):
    def one(a, b):
        return lax.dot_general(a, b, (contract, ((), ())), preferred_element_type=jnp.float32)

    return one(first[0], second[0]) + (one(first[0], second[1]) + one(first[1], second[0]))


def call(kernel, outs, scalars, *arrays, flops=0):
    moved = sum(a.size * a.dtype.itemsize for a in arrays)
    return pl.pallas_call(
        kernel,
        out_shape=outs,
        in_specs=[pl.BlockSpec(memory_space=pltpu.SMEM)] + [pl.BlockSpec(memory_space=pltpu.VMEM)] * len(arrays),
        out_specs=jax.tree.map(lambda _: pl.BlockSpec(memory_space=pltpu.VMEM), outs),
        compiler_params=pltpu.CompilerParams(vmem_limit_bytes=32 * 1024 * 1024),
        cost_estimate=pl.CostEstimate(flops=flops, bytes_accessed=moved, transcendentals=0),
    )(jnp.stack([jnp.asarray(s, jnp.int32) for s in scalars]), *arrays)


def shape(*dims, dtype=jnp.float32):
    return jax.ShapeDtypeStruct(dims, dtype)


def split_kernel(ids, mine, theirs, *refs):
    tiles, (kept_high, kept_low, given_high, given_low) = refs[:-4], refs[-4:]
    half = mine.shape[1]

    def store(place, kept, given):
        kept_high[place], kept_low[place] = split(kept)
        given_high[place], given_low[place] = split(given)

    store(ids[0], mine[...], theirs[...])
    for m, tile in enumerate(tiles):
        store(ids[m + 1], tile[:, :half], tile[:, half:])


def add_products(ids, first_id, lefts, sides, starts, outs):
    height, half = outs[0].shape

    def step(i, carry):
        rows = pl.ds(pl.multiple_of(i * half, half), half)
        totals = [start[rows, :] if start is not None else None for start in starts]
        for j, left in enumerate(lefts):
            parts = split(left[rows, :])
            for s, (high, low) in enumerate(sides):
                k = ids[first_id + j]
                term = dot(parts, (high[k], low[k]))
                totals[s] = term if totals[s] is None else totals[s] + term
        for out, total in zip(outs, totals):
            out[rows, :] = total
        return carry

    lax.fori_loop(0, height // half, step, 0)


def products_kernel(count, sides, started, ids, *refs):
    parts, refs = refs[: 2 * sides], refs[2 * sides :]
    lefts, refs = refs[:count], refs[count:]
    starts, outs = (refs[:sides], refs[sides:]) if started else ([None] * sides, refs)
    add_products(ids, 0, lefts, [parts[2 * s : 2 * s + 2] for s in range(sides)], starts, outs)


def products(ids, lefts, sides, starts=None):
    height, half = lefts[0].shape
    kernel = functools.partial(products_kernel, len(lefts), len(sides), starts is not None)
    flops = 6 * height * half * half * len(lefts) * len(sides)
    args = [part for side in sides for part in side] + list(lefts) + list(starts or [])
    return call(kernel, [shape(height, half)] * len(sides), ids, *args, flops=flops)


def last_kernel(others, downs, ids, high, low, *refs):
    on_line, on_plane = refs[:others], refs[others : others + downs]
    start, out = refs[others + downs :]

    @pl.when(ids[0] == 0)
    def _():
        add_products(ids, 1, on_line, [(high, low)], [start], [out])

    @pl.when(ids[0] == 1)
    def _():
        add_products(ids, 1 + others, on_plane, [(high, low)], [start], [out])


def square_kernel(ids, kept, received, mask, weights, square, given, sums):
    half = kept.shape[1]
    product = kept[...] + received[...]
    square[...] = product * mask[...]
    column = weights[...]
    sums[...] = jnp.zeros_like(sums)
    sums[0:1, :] = jnp.sum(product * column, axis=0, keepdims=True)
    sums[1:2, :] = jnp.sum(square[...] * column, axis=0, keepdims=True)
    given[...] = square[pl.ds(pl.multiple_of((1 - ids[0]) * half, half), half), :]


def turn_kernel(ids, square, theirs, out):
    half = square.shape[1]
    own = pl.ds(pl.multiple_of(ids[0] * half, half), half)
    other = pl.ds(pl.multiple_of((1 - ids[0]) * half, half), half)
    out[own, :] = square[own, :].T
    out[other, :] = theirs[...].T


def diagonal_kernel(ids, *refs):
    lefts, (given, kept) = refs[:-2], refs[-2:]
    height, half = given.shape
    for out, which in ((given, 1 - ids[0]), (kept, ids[0])):
        wanted = pl.ds(pl.multiple_of(which * half, half), half)

        def step(i, carry):
            rows = pl.ds(pl.multiple_of(i * half, half), half)
            out[rows, :] = sum(dot(split(left[rows, :]), split(left[wanted, :]), ROW_BY_ROW) for left in lefts)
            return carry

        lax.fori_loop(0, height // half, step, 0)


def early_kernel(ids, *refs):
    parts, (square, kept, received, mask), outs, diagonal = refs[:4], refs[4:8], refs[8:10], refs[10]
    diagonal[...] = (kept[...] + received[...]) * mask[...]
    add_products(ids, 0, [square, diagonal], [parts[:2], parts[2:]], [None, None], outs)


def check_kernel(ids, *refs):
    parts, rows, (kept, given) = refs[:4], refs[4:-2], refs[-2:]
    for out, (high, low) in ((kept, parts[:2]), (given, parts[2:])):
        out[...] = sum(dot(split(row[...]), (high[ids[j]], low[ids[j]])) for j, row in enumerate(rows))


def make_body(panels, columns):
    assert columns == 2 * panels and panels & (panels - 1) == 0

    def flat(r, z, core):
        return r * columns + 2 * z + core

    def send(value, target):
        pairs = []
        for r in range(panels):
            for z in range(panels):
                to = target(r, z)
                if to is not None:
                    pairs += [(flat(r, z, core), flat(*to, core)) for core in (0, 1)]
        return lax.ppermute(value, ("row", "col"), pairs)

    def swap_core(value):
        return lax.ppermute(value, "col", [(c, c ^ 1) for c in range(columns)])

    def ring(step):
        return lambda r, z: (r, (z + step) % panels)

    def others_ring(step):
        def target(r, z):
            if z == r:
                return None
            line = [q for q in range(panels) if q != r]
            return (r, line[(line.index(z) + step) % len(line)])

        return target

    def across(m):
        return lambda r, z: (r ^ m, z)

    def to_diagonal(m):
        return lambda r, z: (r ^ m, z) if r ^ m == z else None

    def from_diagonal(m):
        return lambda r, z: (r, r ^ m) if r == z else None

    def row_sum(value):
        m = 1
        while m < panels:
            value = value + send(value, across(m))
            m *= 2
        return value

    def gather_ring(value, ring_of, count):
        got = {0: value}
        got[1] = send(value, ring_of(1))
        for j in range(count - 1, count // 2, -1):
            got[j] = send(got[(j + 1) % count], ring_of(-1))
        for j in range(2, count // 2 + 1):
            got[j] = send(got[j - 1], ring_of(1))
        return got

    def body(density, pattern, weights):
        r = lax.axis_index("row")
        c = lax.axis_index("col")
        z, core = c // 2, c % 2
        height, half = density.shape
        block_mask = expand_mask(pattern)

        left = gather_ring(density, ring, panels)
        mine = lax.dynamic_slice_in_dim(density, core * half, half, 0)
        theirs = swap_core(lax.dynamic_slice_in_dim(density, (1 - core) * half, half, 0))
        own = jnp.concatenate([mine, theirs], axis=1)
        own_later, pattern_later, _ = lax.optimization_barrier((own, pattern, left[1]))
        tiles = [send(own if m & (m - 1) == 0 else own_later, across(m)) for m in range(1, panels)]
        diagonal_pattern = sum(send(pattern_later, from_diagonal(m)) for m in range(1, panels))
        diagonal_mask = expand_mask(diagonal_pattern)

        part = shape(panels, half, half, dtype=jnp.bfloat16)
        right = call(split_kernel, [part] * 4, [r ^ m for m in range(panels)], mine, theirs, *tiles)
        kept, given = right[:2], right[2:]

        last = panels // 2
        early = [j for j in range(panels) if j != last]
        starts = products([(z - j) % panels for j in early], [left[j] for j in early], [kept, given])
        at = [(z - last) % panels]
        given_sum = products(at, [left[last]], [given], starts[1:])[0]
        kept_sum = products(at, [left[last]], [kept], starts[:1])[0]
        received = swap_core(given_sum)
        square, quarter, sums = call(
            square_kernel,
            [shape(height, half), shape(half, half), shape(8, half)],
            [core],
            kept_sum,
            received,
            block_mask,
            weights[:, None],
        )

        others = gather_ring(square, others_ring, panels - 1)
        rows = call(turn_kernel, shape(height, half), [core], square, swap_core(quarter))
        down = [send(rows, to_diagonal(m)) for m in range(1, panels)]

        sums = row_sum(sums)
        all_sums = gather_ring(sums, ring, panels)
        check = call(
            check_kernel,
            [shape(8, half)] * 2,
            [(z - j) % panels for j in range(panels)],
            *right,
            *[all_sums[j] for j in range(panels)],
        )
        second_check = check[0] + swap_core(check[1])

        diagonal_given, diagonal_kept = call(
            diagonal_kernel,
            [shape(height, half)] * 2,
            [core],
            *[left[j] for j in range(panels)],
            flops=12 * height * half * half * panels,
        )
        cube = call(
            lambda *refs: early_kernel(*refs),
            [shape(height, half)] * 2 + [shape(height, half)],
            [z, r],
            *right,
            square,
            diagonal_kept,
            swap_core(diagonal_given),
            diagonal_mask,
            flops=24 * height * half * half,
        )

        place = z - (z > r).astype(z.dtype)
        ids = [(z == r).astype(jnp.int32)]
        for j in range(1, panels - 1):
            q = (place - j) % (panels - 1)
            ids.append(q + (q >= r).astype(q.dtype))
        ids += [r ^ m for m in range(1, panels)]
        on_line = [others[j] for j in range(1, panels - 1)]

        def finish(side, start):
            kernel = functools.partial(last_kernel, len(on_line), len(down))
            flops = 6 * height * half * half * len(on_line)
            return call(kernel, shape(height, half), ids, *side, *on_line, *down, start, flops=flops)

        given_cube = finish(given, cube[1])
        kept_cube = finish(kept, cube[0])
        cube_term = block_mask * (kept_cube + swap_core(given_cube))
        checks = jnp.concatenate([sums[:1], second_check[1:2]], axis=0)
        return 3.0 * square - 2.0 * cube_term, checks

    return body


def solution(mesh):
    in_specs = (P("row", "col"), P("row", "col"), P("row"))
    out_specs = (P("row", "col"), P(None, "col"))
    body = make_body(mesh.shape["row"], mesh.shape["col"])
    return jax.shard_map(body, mesh=mesh, in_specs=in_specs, out_specs=out_specs, check_vma=False)
```

```python
import functools

import jax
import jax.numpy as jnp
from jax import lax
from jax.experimental import pallas as pl
from jax.experimental.pallas import tpu as pltpu
from jax.sharding import PartitionSpec as P

BLK = 64
ROWS, LANES = 8, 128
VMEM_BYTES = 24 * 1024 * 1024
ROW_BY_COLUMN = ((1,), (0,))
ROW_BY_ROW = ((1,), (1,))
COLUMN_BY_COLUMN = ((0,), (0,))

CORE, DOWN, ROW, COLUMN, BACK, LISTS = range(6)


def parts(value):
    high = value.astype(jnp.bfloat16)
    return high, (value - high.astype(jnp.float32)).astype(jnp.bfloat16)


def first(value, axis):
    high, low = parts(value)
    return jnp.concatenate([high, high, low], axis=axis)


def second(value, axis):
    high, low = parts(value)
    return jnp.concatenate([high, low, high], axis=axis)


def dot(a, b, contract=ROW_BY_COLUMN):
    return lax.dot_general(a, b, (contract, ((), ())), preferred_element_type=jnp.float32)


def call(kernel, outs, ids, *arrays, placed=0, scratch=()):
    copied = len(arrays) - placed
    held = [pltpu.VMEM(a.shape, a.dtype) for a in arrays[:copied]]
    n_outs = len(jax.tree.leaves(outs))

    def body(ids_ref, *refs):
        sources, rest, own = refs[:copied], refs[copied : len(arrays) + n_outs], refs[len(arrays) + n_outs :]
        targets, sems, own = own[:copied], own[copied], own[copied + 1 :]
        copies = [pltpu.make_async_copy(a, b, sems.at[i]) for i, (a, b) in enumerate(zip(sources, targets))]
        for copy in copies:
            copy.start()
        for copy in copies:
            copy.wait()
        kernel(ids_ref, *targets, *rest, *own)

    return pl.pallas_call(
        body,
        out_shape=outs,
        in_specs=[pl.BlockSpec(memory_space=pltpu.SMEM)] + [pl.BlockSpec(memory_space=pl.ANY)] * len(arrays),
        scratch_shapes=held + [pltpu.SemaphoreType.DMA((max(copied, 1),))] + list(scratch),
        compiler_params=pltpu.CompilerParams(vmem_limit_bytes=VMEM_BYTES),
    )(ids, *arrays)


def shape(*dims, dtype=jnp.float32):
    return jax.ShapeDtypeStruct(dims, dtype)


def after(value, *earlier):
    return lax.optimization_barrier((value, *earlier))[0]


def in_half(value, which):
    half = value.shape[1] // 2
    return jnp.where(which == 0, value[:, :half], value[:, half:])


def ones(count, wide, entry):
    dims = [wide, wide]
    dims[entry] = count * BLK
    entries = lax.broadcasted_iota(jnp.int32, dims, entry)
    return (entries // BLK == lax.broadcasted_iota(jnp.int32, dims, 1 - entry)).astype(jnp.bfloat16)


def spread(blocks, half, height):
    rows = dot(ones(half // BLK, blocks.shape[0], 0), blocks.astype(jnp.bfloat16))
    return dot(rows.astype(jnp.bfloat16), ones(height // BLK, blocks.shape[1], 1))


def pack_kernel(core, tile, pattern, packed, mine, other, blocks):
    half, (high, wide) = tile.shape[0], pattern.shape
    packed[:half, :] = tile[...]
    packed[half:, :] = jnp.zeros((ROWS, tile.shape[1]), jnp.float32)

    def unit(rows, columns):
        same = lax.broadcasted_iota(jnp.int32, (rows, columns), 0) == lax.broadcasted_iota(jnp.int32, (rows, columns), 1)
        return same.astype(jnp.bfloat16)

    turned = dot(unit(ROWS, wide), pattern[...].astype(jnp.float32).astype(jnp.bfloat16), ROW_BY_ROW)
    blocks[...] = dot(turned.astype(jnp.bfloat16), unit(high, LANES))
    packed[half:, :LANES] = blocks[...]
    mine[...] = in_half(tile[...], core[0])
    other[:half, :] = in_half(tile[...], 1 - core[0])
    other[half:, :] = jnp.zeros((ROWS, half), jnp.float32)
    other[half:, :LANES] = blocks[...]


def split_kernel(ids, *refs):
    tiles, (kept, given) = refs[:-2], refs[-2:]
    half = kept.shape[1]
    for m, tile in enumerate(tiles):
        kept[ids[LISTS + m]] = first(tile[:, :half], 1)
        given[ids[LISTS + m]] = first(tile[:, half:], 1)


def held_parts(count, half):
    return [pltpu.VMEM((count, half, 3 * half), jnp.bfloat16), pltpu.SemaphoreType.DMA((count,))]


def fetch(sources, held, sems):
    copies = [pltpu.make_async_copy(source, held.at[t], sems.at[t]) for t, source in enumerate(sources)]
    for copy in copies:
        copy.start()
    for copy in copies:
        copy.wait()


def sums_of_products(places, lefts, starts, rights, held, sems):
    half, count = held.shape[1], len(lefts)
    fetch([right.at[place] for right in rights for place in places], held, sems)
    totals = [None if start is None else start[...] for start in starts]
    for j, left in enumerate(lefts):
        value = second(left[:half, :], 0)
        for s in range(len(rights)):
            term = dot(held[s * count + j], value)
            totals[s] = term if totals[s] is None else totals[s] + term
    return totals


def early_products_kernel(early, line_at, ids, *refs):
    count = len(early)
    lefts, rights, outs, (held, sems) = refs[:count], refs[count : count + 2], refs[count + 2 : count + 4], refs[count + 4 :]
    places = [ids[line_at + j] for j in early]
    for out, total in zip(outs, sums_of_products(places, lefts, [None, None], rights, held, sems)):
        out[...] = total


def last_product_kernel(place, ids, left, start_kept, start_given, right_kept, right_given, kept, given, held, sems):
    height = kept.shape[1]
    starts = [start_kept, start_given]
    kept_sum, given_sum = sums_of_products([ids[place]], [left], starts, [right_kept, right_given], held, sems)
    kept[...] = kept_sum
    given[:, :height] = given_sum
    given[:, height:] = in_half(kept_sum, 1 - ids[CORE])


def square_kernel(ids, kept, given, received, blocks, their_blocks, weights, *outs):
    half, height = kept.shape
    square, sums, outs = outs[0], outs[1], outs[2:]
    product = kept[...] + received[:, :height]
    square[...] = product * spread(blocks[...], half, height)
    row = first(jnp.broadcast_to(weights[...], (ROWS, height)), 1)
    sums[...] = jnp.zeros_like(sums)
    sums[0:1, :] = dot(row, second(product, 1), ROW_BY_ROW)[0:1, :]
    other = in_half(given[:, :height], ids[CORE]) + received[:, height:]
    other = (other * in_half(spread(their_blocks[...], half, height), ids[CORE])).T
    own = in_half(square[...], ids[CORE]).T
    for step, out in enumerate(outs):

        @pl.when(ids[DOWN] != step)
        def _():
            out[...] = square[...]

        @pl.when(ids[DOWN] == step)
        def _():
            out[:, :half] = jnp.where(ids[CORE] == 0, own, other)
            out[:, half:] = jnp.where(ids[CORE] == 0, other, own)


def last_kernel(count, place, ids, start, weights, right, *refs):
    sources, out, held, held_sems, tiles, sems = refs[:count], *refs[count:]
    half, height = start.shape

    def copies(t):
        k = jnp.maximum(ids[place + t], 0)
        yield pltpu.make_async_copy(right.at[k], held.at[t], held_sems.at[t])
        yield pltpu.make_async_copy(sources[t], tiles.at[t], sems.at[t])

    for t in range(count):
        for copy in copies(t):
            copy.start()
    out[:half, :] = start[...]
    for t in range(count):
        for copy in copies(t):
            copy.wait()

        @pl.when(ids[place + t] >= 0)
        def _():
            out[:half, :] += dot(held[t], second(tiles[t], 0))

    row = first(jnp.broadcast_to(weights[...], (ROWS, height)), 1)
    out[half:, :] = jnp.zeros((ROWS, height), jnp.float32)
    out[half + 1 : half + 2, :half] = dot(row, second(out[:half, :], 1), ROW_BY_ROW)[1:2, :]


def diagonal_early_kernel(ids, *refs):
    lefts, out = refs[:-1], refs[-1]
    for j, left in enumerate(lefts):
        tile = left[: out.shape[0] // 2, :]
        term = dot(first(tile, 0), second(tile, 0), COLUMN_BY_COLUMN)
        out[...] = term if j == 0 else out[...] + term


def diagonal_kernel(last, ids, start, left, *refs):
    patterns, (given, kept, blocks, whole) = refs[:-4], refs[-4:]
    half = given.shape[0]
    tile = left[:half, :]
    whole[...] = start[...] + dot(first(tile, 0), second(tile, 0), COLUMN_BY_COLUMN)
    given[...] = whole[pl.ds(pl.multiple_of((1 - ids[CORE]) * half, half), half), :]
    kept[...] = whole[pl.ds(pl.multiple_of(ids[CORE] * half, half), half), :]
    blocks[...] = jnp.zeros_like(blocks)
    for j, pattern in enumerate(patterns):

        @pl.when(ids[BACK] == j + 1)
        def _():
            blocks[...] = pattern[...]


def early_kernel(ids, square, kept, received, blocks, *refs):
    rights, outs, (held, sems) = refs[:2], refs[2:4], refs[4:]
    fetch([right.at[place] for right in rights for place in (ids[COLUMN], ids[ROW])], held, sems)
    own = second(square[...], 0)
    diagonal = second((kept[...] + received[...]) * spread(blocks[...], *kept.shape), 0)
    for s, out in enumerate(outs):
        out[...] = dot(held[2 * s], own) + dot(held[2 * s + 1], diagonal)


def purify_kernel(ids, square, kept, received, blocks, out):
    half, height = square.shape
    cube = kept[:half, :] + received[:half, :]
    out[...] = 3.0 * square[...] - 2.0 * (spread(blocks[...], half, height) * cube)


def in_steps(edges):
    sent, got, count = {}, {}, 0
    for source, target in edges:
        count = max(count, sum(e[0] == source for e in edges), sum(e[1] == target for e in edges))
    for source, target in edges:
        free = next(i for i in range(count) if (source, i) not in sent)
        other = next(i for i in range(count) if (target, i) not in got)
        if free != other:
            path, node, at_target, step = [], target, True, free
            while (node, step) in (got if at_target else sent):
                partner = (got if at_target else sent)[node, step]
                path.append((partner, node, step) if at_target else (node, partner, step))
                node, at_target, step = partner, not at_target, free + other - step
            for u, v, step in path:
                del sent[u, step], got[v, step]
            for u, v, step in path:
                sent[u, free + other - step], got[v, free + other - step] = v, u
        sent[source, free], got[target, free] = target, source
    return count, sent, got


def make_body(panels, columns):
    assert columns == 2 * panels and panels & (panels - 1) == 0
    chips = [(r, z) for r in range(panels) for z in range(panels)]

    edges = [((r, z), (r, q)) for r, z in chips for q in range(panels) if z != r and q != r and q != z]
    edges += [((r, z), (z, z)) for r, z in chips if z != r]
    steps, sent, got = in_steps(edges)
    down_step = [[-1] * panels for _ in range(panels)]
    tile_got = [[[-1] * steps for _ in range(panels)] for _ in range(panels)]
    for ((r, z), step), target in sent.items():
        if target[0] != r:
            down_step[r][z] = step
    for ((r, z), step), source in got.items():
        tile_got[r][z][step] = source[1] if source[0] == r else source[0]

    def send(value, target):
        pairs = []
        for r, z in chips:
            to = target(r, z)
            if to is not None:
                pairs += [(r * columns + 2 * z + core, to[0] * columns + 2 * to[1] + core) for core in (0, 1)]
        return lax.ppermute(value, ("row", "col"), pairs)

    def swap_core(value):
        return lax.ppermute(value, "col", [(c, c ^ 1) for c in range(columns)])

    def ring(step):
        return lambda r, z: (r, (z + step) % panels)

    def across(m):
        return lambda r, z: (r ^ m, z)

    def step_target(step, r, z):
        return sent.get(((r, z), step))

    powers = [1 << i for i in range(panels.bit_length() - 1)]

    def body(density, pattern, weights):
        r = lax.axis_index("row")
        c = lax.axis_index("col")
        z, core = c // 2, c % 2
        tile = density.T
        half, height = tile.shape

        scalars = [core, jnp.asarray(down_step)[r, z], r, z, (z - r) % panels]
        scalars += [r ^ m for m in range(panels)] + [(z - j) % panels for j in range(panels)]
        scalars += list(jnp.asarray(tile_got)[r, z])
        ids = jnp.stack([jnp.asarray(s, jnp.int32) for s in scalars])
        line_at, steps_at = LISTS + panels, LISTS + 2 * panels

        packed, mine, other, blocks = call(
            pack_kernel,
            [shape(half + ROWS, height), shape(half, half), shape(half + ROWS, half), shape(ROWS, LANES)],
            jnp.asarray(core, jnp.int32)[None],
            tile,
            pattern,
        )
        left = {0: packed, 1: send(packed, ring(1))}
        theirs = swap_core(other)
        own = jnp.concatenate([mine, theirs[:half]], axis=1)
        their_blocks = theirs[half:, :LANES]
        tiles = {m: send(own, across(m)) for m in powers}
        nearest = [tiles[m] for m in powers]
        own_later = after(own, *nearest)
        tiles = [own] + [tiles[m] if m in powers else send(own_later, across(m)) for m in range(1, panels)]
        last = panels // 2 + 1
        for j in range(2, last):
            left[j] = send(left[j - 1], ring(1))
        for j in range(panels - 1, last - 1, -1):
            left[j] = send(after(packed, *nearest) if j == panels - 1 else left[j + 1], ring(-1))

        part = shape(panels, half, 3 * half, dtype=jnp.bfloat16)
        kept, given = call(split_kernel, [part] * 2, ids, *tiles)

        early = [j for j in range(panels) if j != last]
        starts = call(
            functools.partial(early_products_kernel, early, line_at),
            [shape(half, height)] * 2,
            ids,
            *[left[j] for j in early],
            kept,
            given,
            placed=2,
            scratch=held_parts(2 * len(early), half),
        )
        diagonal_start = call(diagonal_early_kernel, shape(height, height), ids, *[left[j] for j in early])
        kept_sum, given_sum = call(
            functools.partial(last_product_kernel, line_at + last),
            [shape(half, height), shape(half, height + half)],
            ids,
            left[last],
            *starts,
            kept,
            given,
            placed=2,
            scratch=held_parts(2, half),
        )
        square, sums, *rows = call(
            square_kernel,
            [shape(half, height), shape(ROWS, half)] + [shape(half, height)] * steps,
            ids,
            kept_sum,
            given_sum,
            swap_core(given_sum),
            blocks,
            their_blocks,
            weights[None, :],
        )

        arrived = [send(rows[step], functools.partial(step_target, step)) for step in range(steps)]
        diagonal_given, diagonal_kept, diagonal_blocks = call(
            functools.partial(diagonal_kernel, last),
            [shape(half, height)] * 2 + [shape(ROWS, LANES)],
            ids,
            after(diagonal_start, rows[0]),
            left[last],
            *[left[j][half:, :LANES] for j in range(1, panels)],
            scratch=[pltpu.VMEM((2 * half, height), jnp.float32)],
        )
        cube = call(
            early_kernel,
            [shape(half, height)] * 2,
            ids,
            square,
            diagonal_kept,
            swap_core(diagonal_given),
            diagonal_blocks,
            kept,
            given,
            placed=2,
            scratch=held_parts(4, half),
        )

        held = [pltpu.VMEM((steps, half, height), jnp.float32), pltpu.SemaphoreType.DMA((steps,))]

        def finish(side, start):
            kernel = functools.partial(last_kernel, steps, steps_at)
            scratch = held_parts(steps, half) + held
            arrays = [start, weights[None, :], side, *arrived]
            return call(kernel, shape(half + ROWS, height), ids, *arrays, placed=steps + 1, scratch=scratch)

        given_cube = finish(given, cube[1])
        kept_cube = finish(kept, cube[0])
        received = swap_core(given_cube)
        sums = sums + kept_cube[half:, :half] + received[half:, :half]
        for m in powers:
            sums = sums + send(sums, across(m))
        purified = call(purify_kernel, shape(half, height), ids, square, kept_cube, received, blocks)
        return purified.T, sums[:2]

    return body


def solution(mesh):
    in_specs = (P("row", "col"), P("row", "col"), P("row"))
    out_specs = (P("row", "col"), P(None, "col"))
    body = make_body(mesh.shape["row"], mesh.shape["col"])
    return jax.shard_map(body, mesh=mesh, in_specs=in_specs, out_specs=out_specs, check_vma=False)
```

```python
import functools

import jax
import jax.numpy as jnp
from jax import lax
from jax.experimental import pallas as pl
from jax.experimental.pallas import tpu as pltpu
from jax.sharding import PartitionSpec as P

BLK = 64
ROWS, LANES = 8, 128
VMEM_BYTES = 24 * 1024 * 1024
ROW_BY_COLUMN = ((1,), (0,))
ROW_BY_ROW = ((1,), (1,))
COLUMN_BY_COLUMN = ((0,), (0,))

CORE, DOWN, ROW, COLUMN, BACK, LISTS = range(6)


def parts(value):
    high = value.astype(jnp.bfloat16)
    return high, (value - high.astype(jnp.float32)).astype(jnp.bfloat16)


def first(value, axis):
    high, low = parts(value)
    return jnp.concatenate([high, high, low], axis=axis)


def second(value, axis):
    high, low = parts(value)
    return jnp.concatenate([high, low, high], axis=axis)


def dot(a, b, contract=ROW_BY_COLUMN):
    return lax.dot_general(a, b, (contract, ((), ())), preferred_element_type=jnp.float32)


def call(kernel, outs, ids, *arrays, placed=0, scratch=()):
    pieces, held, homes = [], [], []
    for array in arrays[: len(arrays) - placed]:
        array = array if isinstance(array, list) else [array]
        rows = [a.shape[0] for a in array]
        homes += [(len(held), sum(rows[:i]), n, len(array) > 1) for i, n in enumerate(rows)]
        held.append(pltpu.VMEM((sum(rows), *array[0].shape[1:]), array[0].dtype))
        pieces += array
    arrays = pieces + list(arrays[len(arrays) - placed :])
    copied = len(pieces)
    n_outs = len(jax.tree.leaves(outs))

    def body(ids_ref, *refs):
        sources, rest, own = refs[:copied], refs[copied : len(arrays) + n_outs], refs[len(arrays) + n_outs :]
        targets, sems, own = own[: len(held)], own[len(held)], own[len(held) + 1 :]
        copies = []
        for i, (source, (home, start, n, part)) in enumerate(zip(sources, homes)):
            target = targets[home].at[start : start + n] if part else targets[home]
            copies.append(pltpu.make_async_copy(source, target, sems.at[i]))
        for copy in copies:
            copy.start()
        for copy in copies:
            copy.wait()
        kernel(ids_ref, *targets, *rest, *own)

    return pl.pallas_call(
        body,
        out_shape=outs,
        in_specs=[pl.BlockSpec(memory_space=pltpu.SMEM)] + [pl.BlockSpec(memory_space=pl.ANY)] * len(arrays),
        scratch_shapes=held + [pltpu.SemaphoreType.DMA((max(copied, 1),))] + list(scratch),
        compiler_params=pltpu.CompilerParams(vmem_limit_bytes=VMEM_BYTES),
    )(ids, *arrays)


def shape(*dims, dtype=jnp.float32):
    return jax.ShapeDtypeStruct(dims, dtype)


def after(value, *earlier):
    return lax.optimization_barrier((value, *earlier))[0]


def in_half(value, which):
    half = value.shape[1] // 2
    return jnp.where(which == 0, value[:, :half], value[:, half:])


def ones(count, wide, entry):
    dims = [wide, wide]
    dims[entry] = count * BLK
    entries = lax.broadcasted_iota(jnp.int32, dims, entry)
    return (entries // BLK == lax.broadcasted_iota(jnp.int32, dims, 1 - entry)).astype(jnp.bfloat16)


def spread(blocks, half, height):
    rows = dot(ones(half // BLK, blocks.shape[0], 0), blocks.astype(jnp.bfloat16))
    return dot(rows.astype(jnp.bfloat16), ones(height // BLK, blocks.shape[1], 1))


def pack_kernel(core, tile, pattern, packed, mine, other, blocks):
    half, (wide, high) = tile.shape[0], pattern.shape
    packed[:half, :] = tile[...]
    packed[half:, :] = jnp.zeros((ROWS, tile.shape[1]), jnp.float32)

    def unit(rows, columns):
        same = lax.broadcasted_iota(jnp.int32, (rows, columns), 0) == lax.broadcasted_iota(jnp.int32, (rows, columns), 1)
        return same.astype(jnp.bfloat16)

    rows = dot(unit(ROWS, wide), pattern[...].astype(jnp.float32).astype(jnp.bfloat16))
    blocks[...] = dot(rows.astype(jnp.bfloat16), unit(high, LANES))
    packed[half:, :LANES] = blocks[...]
    mine[...] = in_half(tile[...], core[0])
    other[:half, :] = in_half(tile[...], 1 - core[0])
    other[half:, :] = jnp.zeros((ROWS, half), jnp.float32)
    other[half:, :LANES] = blocks[...]


def split_kernel(ids, *refs):
    tiles, (kept, given) = refs[:-2], refs[-2:]
    half = kept.shape[1]
    for m, tile in enumerate(tiles):
        kept[ids[LISTS + m]] = first(tile[:, :half], 1)
        given[ids[LISTS + m]] = first(tile[:, half:], 1)


def held_parts(count, half):
    return [pltpu.VMEM((count, half, 3 * half), jnp.bfloat16), pltpu.SemaphoreType.DMA((count,))]


def fetch(sources, held, sems):
    copies = [pltpu.make_async_copy(source, held.at[t], sems.at[t]) for t, source in enumerate(sources)]
    for copy in copies:
        copy.start()
    for copy in copies:
        copy.wait()


def sums_of_products(places, lefts, starts, rights, held, sems):
    half, count = held.shape[1], len(lefts)
    fetch([right.at[place] for right in rights for place in places], held, sems)
    totals = [None if start is None else start[...] for start in starts]
    for j, left in enumerate(lefts):
        value = second(left[:half, :], 0)
        for s in range(len(rights)):
            term = dot(held[s * count + j], value)
            totals[s] = term if totals[s] is None else totals[s] + term
    return totals


def early_products_kernel(early, line_at, ids, *refs):
    count = len(early)
    lefts, rights, outs, (held, sems) = refs[:count], refs[count : count + 2], refs[count + 2 : count + 4], refs[count + 4 :]
    places = [ids[line_at + j] for j in early]
    for out, total in zip(outs, sums_of_products(places, lefts, [None, None], rights, held, sems)):
        out[...] = total


def last_product_kernel(place, ids, left, start_kept, start_given, right_kept, right_given, kept, given, held, sems):
    height = kept.shape[1]
    starts = [start_kept, start_given]
    kept_sum, given_sum = sums_of_products([ids[place]], [left], starts, [right_kept, right_given], held, sems)
    kept[...] = kept_sum
    given[:, :height] = given_sum
    given[:, height:] = in_half(kept_sum, 1 - ids[CORE])


def square_kernel(ids, kept, given, received, blocks, theirs, *refs):
    half, height = kept.shape
    square, outs, (their_blocks, sem) = refs[0], refs[1:-2], refs[-2:]
    copy = pltpu.make_async_copy(theirs.at[half:, :LANES], their_blocks, sem)
    copy.start()
    square[...] = (kept[...] + received[:, :height]) * spread(blocks[...], half, height)
    other = in_half(given[:, :height], ids[CORE]) + received[:, height:]
    copy.wait()
    other = (other * in_half(spread(their_blocks[...], half, height), ids[CORE])).T
    own = in_half(square[...], ids[CORE]).T
    for step, out in enumerate(outs):

        @pl.when(ids[DOWN] != step)
        def _():
            out[...] = square[...]

        @pl.when(ids[DOWN] == step)
        def _():
            out[:, :half] = jnp.where(ids[CORE] == 0, own, other)
            out[:, half:] = jnp.where(ids[CORE] == 0, other, own)


def check_sums(weights, value):
    column = jnp.sum(value * weights[...], axis=1, keepdims=True)
    return jnp.broadcast_to(column, (value.shape[0], LANES)).T[:ROWS, :]


def in_row(value, row):
    return jnp.where(lax.broadcasted_iota(jnp.int32, value.shape, 0) == row, value, 0.0)


def last_kernel(count, place, is_kept, ids, start, weights, *refs):
    if is_kept:
        square, blocks, *refs = refs
    right, *refs = refs
    if not is_kept:
        theirs, *refs = refs
    sources, out, held, held_sems, tiles, sems, *refs = refs[:count], *refs[count:]
    half, height = start.shape

    def copies(t):
        k = jnp.maximum(ids[place + t], 0)
        yield pltpu.make_async_copy(right.at[k], held.at[t], held_sems.at[t])
        yield pltpu.make_async_copy(sources[t], tiles.at[t], sems.at[t])

    if not is_kept:
        blocks, sem = refs
        copy = pltpu.make_async_copy(theirs.at[half:, :LANES], blocks, sem)
        copy.start()
        copy.wait()
    for t in range(count):
        for copy in copies(t):
            copy.start()
    out[:half, :] = start[...]
    for t in range(count):
        for copy in copies(t):
            copy.wait()

        @pl.when(ids[place + t] >= 0)
        def _():
            out[:half, :] += dot(held[t], second(tiles[t], 0))

    out[half:, :] = jnp.zeros((ROWS, height), jnp.float32)
    out[half:, :half] = in_row(check_sums(weights, out[:half, :]), 1)
    cube_term = spread(blocks[...], half, height) * out[:half, :]
    out[:half, :] = 3.0 * square[...] - 2.0 * cube_term if is_kept else -2.0 * cube_term


def diagonal_early_kernel(ids, *refs):
    lefts, out = refs[:-1], refs[-1]
    for j, left in enumerate(lefts):
        tile = left[: out.shape[0] // 2, :]
        term = dot(first(tile, 0), second(tile, 0), COLUMN_BY_COLUMN)
        out[...] = term if j == 0 else out[...] + term


def diagonal_kernel(ids, start, left, *refs):
    tiles, (given, kept, blocks, whole, held, sem) = refs[:-6], refs[-6:]
    half = given.shape[0]
    held[...] = jnp.zeros_like(held)
    for j, source in enumerate(tiles):

        @pl.when(ids[BACK] == j + 1)
        def _():
            copy = pltpu.make_async_copy(source.at[half:, :LANES], held, sem)
            copy.start()
            copy.wait()

    blocks[...] = held[...]
    tile = left[:half, :]
    whole[...] = start[...] + dot(first(tile, 0), second(tile, 0), COLUMN_BY_COLUMN)
    given[...] = whole[pl.ds(pl.multiple_of((1 - ids[CORE]) * half, half), half), :]
    kept[...] = whole[pl.ds(pl.multiple_of(ids[CORE] * half, half), half), :]


def early_kernel(ids, square, kept, received, blocks, kept_sum, received_sum, weights, *refs):
    rights, outs, (sums, held, sems) = refs[:2], refs[2:4], refs[4:]
    height = square.shape[1]
    fetch([right.at[place] for right in rights for place in (ids[COLUMN], ids[ROW])], held, sems)
    own = second(square[...], 0)
    diagonal = second((kept[...] + received[...]) * spread(blocks[...], *kept.shape), 0)
    for s, out in enumerate(outs):
        out[...] = dot(held[2 * s], own) + dot(held[2 * s + 1], diagonal)
    sums[...] = in_row(check_sums(weights, kept_sum[...] + received_sum[:, :height]), 0)


def in_steps(edges):
    sent, got, count = {}, {}, 0
    for source, target in edges:
        count = max(count, sum(e[0] == source for e in edges), sum(e[1] == target for e in edges))
    for source, target in edges:
        free = next(i for i in range(count) if (source, i) not in sent)
        other = next(i for i in range(count) if (target, i) not in got)
        if free != other:
            path, node, at_target, step = [], target, True, free
            while (node, step) in (got if at_target else sent):
                partner = (got if at_target else sent)[node, step]
                path.append((partner, node, step) if at_target else (node, partner, step))
                node, at_target, step = partner, not at_target, free + other - step
            for u, v, step in path:
                del sent[u, step], got[v, step]
            for u, v, step in path:
                sent[u, free + other - step], got[v, free + other - step] = v, u
        sent[source, free], got[target, free] = target, source
    return count, sent, got


def make_body(panels, columns):
    assert columns == 2 * panels and panels & (panels - 1) == 0
    chips = [(r, z) for r in range(panels) for z in range(panels)]

    edges = [((r, z), (r, q)) for r, z in chips for q in range(panels) if z != r and q != r and q != z]
    edges += [((r, z), (z, z)) for r, z in chips if z != r]
    steps, sent, got = in_steps(edges)
    down_step = [[-1] * panels for _ in range(panels)]
    tile_got = [[[-1] * steps for _ in range(panels)] for _ in range(panels)]
    for ((r, z), step), target in sent.items():
        if target[0] != r:
            down_step[r][z] = step
    for ((r, z), step), source in got.items():
        tile_got[r][z][step] = source[1] if source[0] == r else source[0]

    def send(value, target):
        pairs = []
        for r, z in chips:
            to = target(r, z)
            if to is not None:
                pairs += [(r * columns + 2 * z + core, to[0] * columns + 2 * to[1] + core) for core in (0, 1)]
        return lax.ppermute(value, ("row", "col"), pairs)

    def swap_core(value):
        return lax.ppermute(value, "col", [(c, c ^ 1) for c in range(columns)])

    def ring(step):
        return lambda r, z: (r, (z + step) % panels)

    def across(m):
        return lambda r, z: (r ^ m, z)

    def step_target(step, r, z):
        return sent.get(((r, z), step))

    powers = [1 << i for i in range(panels.bit_length() - 1)]

    def body(density, pattern, weights):
        r = lax.axis_index("row")
        c = lax.axis_index("col")
        z, core = c // 2, c % 2
        tile = density.T
        half, height = tile.shape

        scalars = [core, jnp.asarray(down_step)[r, z], r, z, (z - r) % panels]
        scalars += [r ^ m for m in range(panels)] + [(z - j) % panels for j in range(panels)]
        scalars += list(jnp.asarray(tile_got)[r, z])
        ids = jnp.stack([jnp.asarray(s, jnp.int32) for s in scalars])
        line_at, steps_at = LISTS + panels, LISTS + 2 * panels

        packed, mine, other, blocks = call(
            pack_kernel,
            [shape(half + ROWS, height), shape(half, half), shape(half + ROWS, half), shape(ROWS, LANES)],
            jnp.asarray(core, jnp.int32)[None],
            tile,
            pattern.T,
        )
        left = {0: packed, 1: send(packed, ring(1))}
        theirs = swap_core(other)
        own = jnp.concatenate([mine, theirs[:half]], axis=1)
        tiles = {m: send(own, across(m)) for m in powers}
        own_later = after(own, *[tiles[m] for m in powers])
        tiles = [own] + [tiles[m] if m in powers else send(own_later, across(m)) for m in range(1, panels)]
        last = panels // 2 + 1
        for j in range(2, last):
            left[j] = send(left[j - 1], ring(1))
        for j in range(panels - 1, last - 1, -1):
            left[j] = send(after(packed, own) if j == panels - 1 else left[j + 1], ring(-1))

        part = shape(panels, half, 3 * half, dtype=jnp.bfloat16)
        kept, given = call(split_kernel, [part] * 2, ids, *tiles)

        early = [j for j in range(panels) if j != last]
        starts = call(
            functools.partial(early_products_kernel, early, line_at),
            [shape(half, height)] * 2,
            ids,
            *[left[j] for j in early],
            kept,
            given,
            placed=2,
            scratch=held_parts(2 * len(early), half),
        )
        diagonal_start = call(diagonal_early_kernel, shape(height, height), ids, *[left[j] for j in early])
        kept_sum, given_sum = call(
            functools.partial(last_product_kernel, line_at + last),
            [shape(half, height), shape(half, height + half)],
            ids,
            left[last],
            after(starts[0], diagonal_start),
            starts[1],
            kept,
            given,
            placed=2,
            scratch=held_parts(2, half),
        )
        diagonal_given, diagonal_kept, diagonal_blocks = call(
            diagonal_kernel,
            [shape(half, height)] * 2 + [shape(ROWS, LANES)],
            ids,
            diagonal_start,
            left[last],
            *[left[j] for j in range(1, panels)],
            placed=panels - 1,
            scratch=[
                pltpu.VMEM((height, height), jnp.float32),
                pltpu.VMEM((ROWS, LANES), jnp.float32),
                pltpu.SemaphoreType.DMA,
            ],
        )
        received = swap_core(given_sum)
        square, *rows = call(
            square_kernel,
            [shape(half, height)] * (1 + steps),
            ids,
            after(kept_sum, diagonal_given),
            given_sum,
            received,
            blocks,
            theirs,
            placed=1,
            scratch=[pltpu.VMEM((ROWS, LANES), jnp.float32), pltpu.SemaphoreType.DMA],
        )

        arrived = [send(rows[step], functools.partial(step_target, step)) for step in range(steps)]
        *cube, sums = call(
            early_kernel,
            [shape(half, height)] * 2 + [shape(ROWS, half)],
            ids,
            square,
            diagonal_kept,
            swap_core(diagonal_given),
            diagonal_blocks,
            kept_sum,
            received,
            weights[None, :],
            kept,
            given,
            placed=2,
            scratch=held_parts(4, half),
        )

        held = [pltpu.VMEM((steps, half, height), jnp.float32), pltpu.SemaphoreType.DMA((steps,))]

        kernel = functools.partial(last_kernel, steps, steps_at)
        out = shape(half + ROWS, height)
        scratch = held_parts(steps, half) + held
        given_cube = call(
            functools.partial(kernel, False),
            out,
            ids,
            cube[1],
            weights[None, :],
            given,
            theirs,
            *arrived,
            placed=steps + 2,
            scratch=scratch + [pltpu.VMEM((ROWS, LANES), jnp.float32), pltpu.SemaphoreType.DMA],
        )
        kept_cube = call(
            functools.partial(kernel, True),
            out,
            ids,
            cube[0],
            weights[None, :],
            square,
            blocks,
            kept,
            *arrived,
            placed=steps + 1,
            scratch=scratch,
        )
        received = swap_core(given_cube)
        sums = sums + kept_cube[half:, :half] + received[half:, :half]
        for m in powers:
            sums = sums + send(sums, across(m))
        return (kept_cube[:half] + received[:half]).T, sums[:2]

    return body


def solution(mesh):
    in_specs = (P("row", "col"), P("row", "col"), P("row"))
    out_specs = (P("row", "col"), P(None, "col"))
    body = make_body(mesh.shape["row"], mesh.shape["col"])
    return jax.shard_map(body, mesh=mesh, in_specs=in_specs, out_specs=out_specs, check_vma=False)
```

```python
import functools

import jax
import jax.numpy as jnp
from jax import lax
from jax.experimental import pallas as pl
from jax.experimental.pallas import tpu as pltpu
from jax.sharding import PartitionSpec as P

BLK = 64
ROWS, LANES = 8, 128
VMEM_BYTES = 24 * 1024 * 1024
ROW_BY_COLUMN = ((1,), (0,))
ROW_BY_ROW = ((1,), (1,))
COLUMN_BY_COLUMN = ((0,), (0,))

CORE, DOWN, ROW, COLUMN, BACK, LISTS = range(6)


def parts(value):
    high = value.astype(jnp.bfloat16)
    return high, (value - high.astype(jnp.float32)).astype(jnp.bfloat16)


def first(value, axis):
    high, low = parts(value)
    return jnp.concatenate([high, high, low], axis=axis)


def second(value, axis):
    high, low = parts(value)
    return jnp.concatenate([high, low, high], axis=axis)


def dot(a, b, contract=ROW_BY_COLUMN):
    return lax.dot_general(a, b, (contract, ((), ())), preferred_element_type=jnp.float32)


def call(kernel, outs, ids, *arrays, placed=0, scratch=()):
    pieces, held, homes = [], [], []
    for array in arrays[: len(arrays) - placed]:
        array = array if isinstance(array, list) else [array]
        rows = [a.shape[0] for a in array]
        homes += [(len(held), sum(rows[:i]), n, len(array) > 1) for i, n in enumerate(rows)]
        held.append(pltpu.VMEM((sum(rows), *array[0].shape[1:]), array[0].dtype))
        pieces += array
    arrays = pieces + list(arrays[len(arrays) - placed :])
    copied = len(pieces)
    n_outs = len(jax.tree.leaves(outs))

    def body(ids_ref, *refs):
        sources, rest, own = refs[:copied], refs[copied : len(arrays) + n_outs], refs[len(arrays) + n_outs :]
        targets, sems, own = own[: len(held)], own[len(held)], own[len(held) + 1 :]
        copies = []
        for i, (source, (home, start, n, part)) in enumerate(zip(sources, homes)):
            target = targets[home].at[start : start + n] if part else targets[home]
            copies.append(pltpu.make_async_copy(source, target, sems.at[i]))
        for copy in copies:
            copy.start()
        for copy in copies:
            copy.wait()
        kernel(ids_ref, *targets, *rest, *own)

    return pl.pallas_call(
        body,
        out_shape=outs,
        in_specs=[pl.BlockSpec(memory_space=pltpu.SMEM)] + [pl.BlockSpec(memory_space=pl.ANY)] * len(arrays),
        scratch_shapes=held + [pltpu.SemaphoreType.DMA((max(copied, 1),))] + list(scratch),
        compiler_params=pltpu.CompilerParams(vmem_limit_bytes=VMEM_BYTES),
    )(ids, *arrays)


def shape(*dims, dtype=jnp.float32):
    return jax.ShapeDtypeStruct(dims, dtype)


def after(value, *earlier):
    return lax.optimization_barrier((value, *earlier))[0]


def in_half(value, which):
    half = value.shape[1] // 2
    return jnp.where(which == 0, value[:, :half], value[:, half:])


def ones(count, wide, entry):
    dims = [wide, wide]
    dims[entry] = count * BLK
    entries = lax.broadcasted_iota(jnp.int32, dims, entry)
    return (entries // BLK == lax.broadcasted_iota(jnp.int32, dims, 1 - entry)).astype(jnp.bfloat16)


def spread(blocks, half, height):
    rows = dot(ones(half // BLK, blocks.shape[0], 0), blocks.astype(jnp.bfloat16))
    return dot(rows.astype(jnp.bfloat16), ones(height // BLK, blocks.shape[1], 1))


def pack_kernel(core, tile, pattern, packed, mine, other, blocks):
    half, (wide, high) = tile.shape[0], pattern.shape
    packed[:half, :] = tile[...]
    packed[half:, :] = jnp.zeros((ROWS, tile.shape[1]), jnp.float32)

    def unit(rows, columns):
        same = lax.broadcasted_iota(jnp.int32, (rows, columns), 0) == lax.broadcasted_iota(jnp.int32, (rows, columns), 1)
        return same.astype(jnp.bfloat16)

    rows = dot(unit(ROWS, wide), pattern[...].astype(jnp.float32).astype(jnp.bfloat16))
    blocks[...] = dot(rows.astype(jnp.bfloat16), unit(high, LANES))
    packed[half:, :LANES] = blocks[...]
    mine[...] = in_half(tile[...], core[0])
    other[:half, :] = in_half(tile[...], 1 - core[0])
    other[half:, :] = jnp.zeros((ROWS, half), jnp.float32)
    other[half:, :LANES] = blocks[...]


def split_kernel(ids, *refs):
    tiles, (kept, given) = refs[:-2], refs[-2:]
    half = kept.shape[1]
    for m, tile in enumerate(tiles):
        kept[ids[LISTS + m]] = first(tile[:, :half], 1)
        given[ids[LISTS + m]] = first(tile[:, half:], 1)


def held_parts(count, half):
    return [pltpu.VMEM((count, half, 3 * half), jnp.bfloat16), pltpu.SemaphoreType.DMA((count,))]


def fetch(sources, held, sems):
    copies = [pltpu.make_async_copy(source, held.at[t], sems.at[t]) for t, source in enumerate(sources)]
    for copy in copies:
        copy.start()
    for copy in copies:
        copy.wait()


def sums_of_products(places, lefts, starts, rights, held, sems):
    half, count = held.shape[1], len(lefts)
    fetch([right.at[place] for right in rights for place in places], held, sems)
    totals = [None if start is None else start[...] for start in starts]
    for j, left in enumerate(lefts):
        value = second(left[:half, :], 0)
        for s in range(len(rights)):
            term = dot(held[s * count + j], value)
            totals[s] = term if totals[s] is None else totals[s] + term
    return totals


def early_products_kernel(early, line_at, ids, *refs):
    count = len(early)
    lefts, rights, outs, (held, sems) = refs[:count], refs[count : count + 2], refs[count + 2 : count + 4], refs[count + 4 :]
    places = [ids[line_at + j] for j in early]
    for out, total in zip(outs, sums_of_products(places, lefts, [None, None], rights, held, sems)):
        out[...] = total


def last_product_kernel(place, ids, left, start_kept, start_given, right_kept, right_given, kept, given, held, sems):
    height = kept.shape[1]
    starts = [start_kept, start_given]
    kept_sum, given_sum = sums_of_products([ids[place]], [left], starts, [right_kept, right_given], held, sems)
    kept[...] = kept_sum
    given[:, :height] = given_sum
    given[:, height:] = in_half(kept_sum, 1 - ids[CORE])


def square_kernel(ids, kept, given, received, blocks, theirs, *refs):
    half, height = kept.shape
    square, outs, (their_blocks, sem) = refs[0], refs[1:-2], refs[-2:]
    copy = pltpu.make_async_copy(theirs.at[half:, :LANES], their_blocks, sem)
    copy.start()
    square[...] = (kept[...] + received[:, :height]) * spread(blocks[...], half, height)
    other = in_half(given[:, :height], ids[CORE]) + received[:, height:]
    copy.wait()
    other = (other * in_half(spread(their_blocks[...], half, height), ids[CORE])).T
    own = in_half(square[...], ids[CORE]).T
    for step, out in enumerate(outs):

        @pl.when(ids[DOWN] != step)
        def _():
            out[...] = square[...]

        @pl.when(ids[DOWN] == step)
        def _():
            out[:, :half] = jnp.where(ids[CORE] == 0, own, other)
            out[:, half:] = jnp.where(ids[CORE] == 0, other, own)


def check_sums(weights, value):
    column = jnp.sum(value * weights[...], axis=1, keepdims=True)
    return jnp.broadcast_to(column, (value.shape[0], LANES)).T[:ROWS, :]


def in_row(value, row):
    return jnp.where(lax.broadcasted_iota(jnp.int32, value.shape, 0) == row, value, 0.0)


def last_kernel(count, place, is_kept, ids, start, weights, *refs):
    if is_kept:
        square, blocks, *refs = refs
    right, *refs = refs
    if not is_kept:
        theirs, *refs = refs
    sources, out, held, held_sems, tiles, sems, *refs = refs[:count], *refs[count:]
    half, height = start.shape

    def copies(t):
        k = jnp.maximum(ids[place + t], 0)
        yield pltpu.make_async_copy(right.at[k], held.at[t], held_sems.at[t])
        yield pltpu.make_async_copy(sources[t], tiles.at[t], sems.at[t])

    if not is_kept:
        blocks, sem = refs
        copy = pltpu.make_async_copy(theirs.at[half:, :LANES], blocks, sem)
        copy.start()
        copy.wait()
    for t in range(count):

        @pl.when(ids[place + t] >= 0)
        def _():
            for copy in copies(t):
                copy.start()

    out[:half, :] = start[...]
    for t in range(count):

        @pl.when(ids[place + t] >= 0)
        def _():
            for copy in copies(t):
                copy.wait()
            out[:half, :] += dot(held[t], second(tiles[t], 0))

    out[half:, :] = jnp.zeros((ROWS, height), jnp.float32)
    out[half:, :half] = in_row(check_sums(weights, out[:half, :]), 1)
    cube_term = spread(blocks[...], half, height) * out[:half, :]
    out[:half, :] = 3.0 * square[...] - 2.0 * cube_term if is_kept else -2.0 * cube_term


def diagonal_early_kernel(ids, *refs):
    lefts, out = refs[:-1], refs[-1]
    for j, left in enumerate(lefts):
        tile = left[: out.shape[0] // 2, :]
        term = dot(first(tile, 0), second(tile, 0), COLUMN_BY_COLUMN)
        out[...] = term if j == 0 else out[...] + term


def diagonal_kernel(ids, start, left, *refs):
    tiles, (given, kept, blocks, whole, held, sem) = refs[:-6], refs[-6:]
    half = given.shape[0]
    held[...] = jnp.zeros_like(held)
    for j, source in enumerate(tiles):

        @pl.when(ids[BACK] == j + 1)
        def _():
            copy = pltpu.make_async_copy(source.at[half:, :LANES], held, sem)
            copy.start()
            copy.wait()

    blocks[...] = held[...]
    tile = left[:half, :]
    whole[...] = start[...] + dot(first(tile, 0), second(tile, 0), COLUMN_BY_COLUMN)
    given[...] = whole[pl.ds(pl.multiple_of((1 - ids[CORE]) * half, half), half), :]
    kept[...] = whole[pl.ds(pl.multiple_of(ids[CORE] * half, half), half), :]


def early_kernel(ids, square, kept, received, blocks, kept_sum, received_sum, weights, *refs):
    rights, outs, (sums, held, sems) = refs[:2], refs[2:4], refs[4:]
    height = square.shape[1]
    fetch([right.at[place] for right in rights for place in (ids[COLUMN], ids[ROW])], held, sems)
    own = second(square[...], 0)
    diagonal = second((kept[...] + received[...]) * spread(blocks[...], *kept.shape), 0)
    for s, out in enumerate(outs):
        out[...] = dot(held[2 * s], own) + dot(held[2 * s + 1], diagonal)
    sums[...] = in_row(check_sums(weights, kept_sum[...] + received_sum[:, :height]), 0)


def in_steps(edges):
    sent, got, count = {}, {}, 0
    for source, target in edges:
        count = max(count, sum(e[0] == source for e in edges), sum(e[1] == target for e in edges))
    for source, target in edges:
        free = next(i for i in range(count) if (source, i) not in sent)
        other = next(i for i in range(count) if (target, i) not in got)
        if free != other:
            path, node, at_target, step = [], target, True, free
            while (node, step) in (got if at_target else sent):
                partner = (got if at_target else sent)[node, step]
                path.append((partner, node, step) if at_target else (node, partner, step))
                node, at_target, step = partner, not at_target, free + other - step
            for u, v, step in path:
                del sent[u, step], got[v, step]
            for u, v, step in path:
                sent[u, free + other - step], got[v, free + other - step] = v, u
        sent[source, free], got[target, free] = target, source
    return count, sent, got


def make_body(panels, columns):
    assert columns == 2 * panels and panels & (panels - 1) == 0
    chips = [(r, z) for r in range(panels) for z in range(panels)]

    edges = [((r, z), (r, q)) for r, z in chips for q in range(panels) if z != r and q != r and q != z]
    edges += [((r, z), (z, z)) for r, z in chips if z != r]
    steps, sent, got = in_steps(edges)
    down_step = [[-1] * panels for _ in range(panels)]
    tile_got = [[[-1] * steps for _ in range(panels)] for _ in range(panels)]
    for ((r, z), step), target in sent.items():
        if target[0] != r:
            down_step[r][z] = step
    for ((r, z), step), source in got.items():
        tile_got[r][z][step] = source[1] if source[0] == r else source[0]

    def send(value, target):
        pairs = []
        for r, z in chips:
            to = target(r, z)
            if to is not None:
                pairs += [(r * columns + 2 * z + core, to[0] * columns + 2 * to[1] + core) for core in (0, 1)]
        return lax.ppermute(value, ("row", "col"), pairs)

    def swap_core(value):
        return lax.ppermute(value, "col", [(c, c ^ 1) for c in range(columns)])

    def ring(step):
        return lambda r, z: (r, (z + step) % panels)

    def across(m):
        return lambda r, z: (r ^ m, z)

    def step_target(step, r, z):
        return sent.get(((r, z), step))

    powers = [1 << i for i in range(panels.bit_length() - 1)]

    def body(density, pattern, weights):
        r = lax.axis_index("row")
        c = lax.axis_index("col")
        z, core = c // 2, c % 2
        tile = density.T
        half, height = tile.shape

        scalars = [core, jnp.asarray(down_step)[r, z], r, z, (z - r) % panels]
        scalars += [r ^ m for m in range(panels)] + [(z - j) % panels for j in range(panels)]
        scalars += list(jnp.asarray(tile_got)[r, z])
        ids = jnp.stack([jnp.asarray(s, jnp.int32) for s in scalars])
        line_at, steps_at = LISTS + panels, LISTS + 2 * panels

        packed, mine, other, blocks = call(
            pack_kernel,
            [shape(half + ROWS, height), shape(half, half), shape(half + ROWS, half), shape(ROWS, LANES)],
            jnp.asarray(core, jnp.int32)[None],
            tile,
            pattern.T,
        )
        left = {0: packed, 1: send(packed, ring(1))}
        theirs = swap_core(other)
        own = jnp.concatenate([mine, theirs[:half]], axis=1)
        tiles = {m: send(own, across(m)) for m in powers}
        own_later = after(own, *[tiles[m] for m in powers])
        tiles = [own] + [tiles[m] if m in powers else send(own_later, across(m)) for m in range(1, panels)]
        last = panels // 2 + 1
        for j in range(2, last):
            left[j] = send(left[j - 1], ring(1))
        for j in range(panels - 1, last - 1, -1):
            left[j] = send(after(packed, own) if j == panels - 1 else left[j + 1], ring(-1))

        part = shape(panels, half, 3 * half, dtype=jnp.bfloat16)
        kept, given = call(split_kernel, [part] * 2, ids, *tiles)

        early = [j for j in range(panels) if j != last]
        starts = call(
            functools.partial(early_products_kernel, early, line_at),
            [shape(half, height)] * 2,
            ids,
            *[left[j] for j in early],
            kept,
            given,
            placed=2,
            scratch=held_parts(2 * len(early), half),
        )
        diagonal_start = call(diagonal_early_kernel, shape(height, height), ids, *[left[j] for j in early])
        kept_sum, given_sum = call(
            functools.partial(last_product_kernel, line_at + last),
            [shape(half, height), shape(half, height + half)],
            ids,
            left[last],
            after(starts[0], diagonal_start),
            starts[1],
            kept,
            given,
            placed=2,
            scratch=held_parts(2, half),
        )
        diagonal_given, diagonal_kept, diagonal_blocks = call(
            diagonal_kernel,
            [shape(half, height)] * 2 + [shape(ROWS, LANES)],
            ids,
            diagonal_start,
            left[last],
            *[left[j] for j in range(1, panels)],
            placed=panels - 1,
            scratch=[
                pltpu.VMEM((height, height), jnp.float32),
                pltpu.VMEM((ROWS, LANES), jnp.float32),
                pltpu.SemaphoreType.DMA,
            ],
        )
        received = swap_core(given_sum)
        square, *rows = call(
            square_kernel,
            [shape(half, height)] * (1 + steps),
            ids,
            after(kept_sum, diagonal_given),
            given_sum,
            received,
            blocks,
            theirs,
            placed=1,
            scratch=[pltpu.VMEM((ROWS, LANES), jnp.float32), pltpu.SemaphoreType.DMA],
        )

        arrived = [send(rows[step], functools.partial(step_target, step)) for step in range(steps)]
        *cube, sums = call(
            early_kernel,
            [shape(half, height)] * 2 + [shape(ROWS, half)],
            ids,
            square,
            diagonal_kept,
            swap_core(diagonal_given),
            diagonal_blocks,
            kept_sum,
            received,
            weights[None, :],
            kept,
            given,
            placed=2,
            scratch=held_parts(4, half),
        )

        held = [pltpu.VMEM((steps, half, height), jnp.float32), pltpu.SemaphoreType.DMA((steps,))]

        kernel = functools.partial(last_kernel, steps, steps_at)
        out = shape(half + ROWS, height)
        scratch = held_parts(steps, half) + held
        given_cube = call(
            functools.partial(kernel, False),
            out,
            ids,
            cube[1],
            weights[None, :],
            given,
            theirs,
            *arrived,
            placed=steps + 2,
            scratch=scratch + [pltpu.VMEM((ROWS, LANES), jnp.float32), pltpu.SemaphoreType.DMA],
        )
        kept_cube = call(
            functools.partial(kernel, True),
            out,
            ids,
            cube[0],
            weights[None, :],
            square,
            blocks,
            kept,
            *arrived,
            placed=steps + 1,
            scratch=scratch,
        )
        received = swap_core(given_cube)
        sums = sums + kept_cube[half:, :half] + received[half:, :half]
        sums = sums + sum(send(sums, across(m)) for m in range(1, panels))
        return (kept_cube[:half] + received[:half]).T, sums[:2]

    return body


def solution(mesh):
    in_specs = (P("row", "col"), P("row", "col"), P("row"))
    out_specs = (P("row", "col"), P(None, "col"))
    body = make_body(mesh.shape["row"], mesh.shape["col"])
    return jax.shard_map(body, mesh=mesh, in_specs=in_specs, out_specs=out_specs, check_vma=False)
```

```python
import functools

import jax
import jax.numpy as jnp
from jax import lax
from jax.experimental import pallas as pl
from jax.experimental.pallas import tpu as pltpu
from jax.sharding import PartitionSpec as P

BLK = 64
ROWS, LANES = 8, 128
VMEM_BYTES = 24 * 1024 * 1024
ROW_BY_COLUMN = ((1,), (0,))
ROW_BY_ROW = ((1,), (1,))
COLUMN_BY_COLUMN = ((0,), (0,))

CORE, DOWN, ROW, COLUMN, BACK, LISTS = range(6)


def parts(value):
    high = value.astype(jnp.bfloat16)
    return high, (value - high.astype(jnp.float32)).astype(jnp.bfloat16)


def first(value, axis):
    high, low = parts(value)
    return jnp.concatenate([high, high, low], axis=axis)


def second(value, axis):
    high, low = parts(value)
    return jnp.concatenate([high, low, high], axis=axis)


def dot(a, b, contract=ROW_BY_COLUMN):
    return lax.dot_general(a, b, (contract, ((), ())), preferred_element_type=jnp.float32)


def call(kernel, outs, ids, *arrays, placed=0, scratch=()):
    pieces, held, homes = [], [], []
    for array in arrays[: len(arrays) - placed]:
        array = array if isinstance(array, list) else [array]
        rows = [a.shape[0] for a in array]
        homes += [(len(held), sum(rows[:i]), n, len(array) > 1) for i, n in enumerate(rows)]
        held.append(pltpu.VMEM((sum(rows), *array[0].shape[1:]), array[0].dtype))
        pieces += array
    arrays = pieces + list(arrays[len(arrays) - placed :])
    copied = len(pieces)
    n_outs = len(jax.tree.leaves(outs))

    def body(ids_ref, *refs):
        sources, rest, own = refs[:copied], refs[copied : len(arrays) + n_outs], refs[len(arrays) + n_outs :]
        targets, sems, own = own[: len(held)], own[len(held)], own[len(held) + 1 :]
        copies = []
        for i, (source, (home, start, n, part)) in enumerate(zip(sources, homes)):
            target = targets[home].at[start : start + n] if part else targets[home]
            copies.append(pltpu.make_async_copy(source, target, sems.at[i]))
        for copy in copies:
            copy.start()
        for copy in copies:
            copy.wait()
        kernel(ids_ref, *targets, *rest, *own)

    return pl.pallas_call(
        body,
        out_shape=outs,
        in_specs=[pl.BlockSpec(memory_space=pltpu.SMEM)] + [pl.BlockSpec(memory_space=pl.ANY)] * len(arrays),
        scratch_shapes=held + [pltpu.SemaphoreType.DMA((max(copied, 1),))] + list(scratch),
        compiler_params=pltpu.CompilerParams(vmem_limit_bytes=VMEM_BYTES),
    )(ids, *arrays)


def shape(*dims, dtype=jnp.float32):
    return jax.ShapeDtypeStruct(dims, dtype)


def after(value, *earlier):
    return lax.optimization_barrier((value, *earlier))[0]


def in_half(value, which):
    half = value.shape[1] // 2
    return jnp.where(which == 0, value[:, :half], value[:, half:])


def ones(count, wide, entry):
    dims = [wide, wide]
    dims[entry] = count * BLK
    entries = lax.broadcasted_iota(jnp.int32, dims, entry)
    return (entries // BLK == lax.broadcasted_iota(jnp.int32, dims, 1 - entry)).astype(jnp.bfloat16)


def spread(blocks, half, height):
    rows = dot(ones(half // BLK, blocks.shape[0], 0), blocks.astype(jnp.bfloat16))
    return dot(rows.astype(jnp.bfloat16), ones(height // BLK, blocks.shape[1], 1))


def pack_kernel(core, tile, pattern, packed, mine, other, blocks):
    half, (wide, high) = tile.shape[0], pattern.shape
    packed[:half, :] = tile[...]
    packed[half:, :] = jnp.zeros((ROWS, tile.shape[1]), jnp.float32)

    def unit(rows, columns):
        same = lax.broadcasted_iota(jnp.int32, (rows, columns), 0) == lax.broadcasted_iota(jnp.int32, (rows, columns), 1)
        return same.astype(jnp.bfloat16)

    rows = dot(unit(ROWS, wide), pattern[...].astype(jnp.float32).astype(jnp.bfloat16))
    blocks[...] = dot(rows.astype(jnp.bfloat16), unit(high, LANES))
    packed[half:, :LANES] = blocks[...]
    mine[...] = in_half(tile[...], core[0])
    other[:half, :] = in_half(tile[...], 1 - core[0])
    other[half:, :] = jnp.zeros((ROWS, half), jnp.float32)
    other[half:, :LANES] = blocks[...]


def split_kernel(ids, *refs):
    tiles, (kept, given) = refs[:-2], refs[-2:]
    half = kept.shape[1]
    for m, tile in enumerate(tiles):
        kept[ids[LISTS + m]] = first(tile[:, :half], 1)
        given[ids[LISTS + m]] = first(tile[:, half:], 1)


def held_parts(count, half):
    return [pltpu.VMEM((count, half, 3 * half), jnp.bfloat16), pltpu.SemaphoreType.DMA((count,))]


def fetch(sources, held, sems):
    copies = [pltpu.make_async_copy(source, held.at[t], sems.at[t]) for t, source in enumerate(sources)]
    for copy in copies:
        copy.start()
    for copy in copies:
        copy.wait()


def sums_of_products(places, lefts, starts, rights, held, sems):
    half, count = held.shape[1], len(lefts)
    fetch([right.at[place] for right in rights for place in places], held, sems)
    totals = [None if start is None else start[...] for start in starts]
    for j, left in enumerate(lefts):
        value = second(left[:half, :], 0)
        for s in range(len(rights)):
            term = dot(held[s * count + j], value)
            totals[s] = term if totals[s] is None else totals[s] + term
    return totals


def early_products_kernel(early, line_at, ids, *refs):
    count = len(early)
    lefts, rights, outs, (held, sems) = refs[:count], refs[count : count + 2], refs[count + 2 : count + 4], refs[count + 4 :]
    places = [ids[line_at + j] for j in early]
    for out, total in zip(outs, sums_of_products(places, lefts, [None, None], rights, held, sems)):
        out[...] = total


def last_product_kernel(place, ids, left, start_kept, start_given, right_kept, right_given, kept, given, held, sems):
    height = kept.shape[1]
    starts = [start_kept, start_given]
    kept_sum, given_sum = sums_of_products([ids[place]], [left], starts, [right_kept, right_given], held, sems)
    kept[...] = kept_sum
    given[:, :height] = given_sum
    given[:, height:] = in_half(kept_sum, 1 - ids[CORE])


def square_kernel(ids, kept, given, received, blocks, theirs, *refs):
    half, height = kept.shape
    square, outs, (their_blocks, sem) = refs[0], refs[1:-2], refs[-2:]
    copy = pltpu.make_async_copy(theirs.at[half:, :LANES], their_blocks, sem)
    copy.start()
    square[...] = (kept[...] + received[:, :height]) * spread(blocks[...], half, height)
    other = in_half(given[:, :height], ids[CORE]) + received[:, height:]
    copy.wait()
    other = (other * in_half(spread(their_blocks[...], half, height), ids[CORE])).T
    own = in_half(square[...], ids[CORE]).T
    for step, out in enumerate(outs):

        @pl.when(ids[DOWN] != step)
        def _():
            out[...] = square[...]

        @pl.when(ids[DOWN] == step)
        def _():
            out[:, :half] = jnp.where(ids[CORE] == 0, own, other)
            out[:, half:] = jnp.where(ids[CORE] == 0, other, own)


def check_sums(weights, value):
    column = jnp.sum(value * weights[...], axis=1, keepdims=True)
    return jnp.broadcast_to(column, (value.shape[0], LANES)).T[:ROWS, :]


def in_row(value, row):
    return jnp.where(lax.broadcasted_iota(jnp.int32, value.shape, 0) == row, value, 0.0)


def last_kernel(count, place, is_kept, ids, start, weights, *refs):
    if is_kept:
        square, blocks, *refs = refs
    right, *refs = refs
    if not is_kept:
        theirs, *refs = refs
    sources, out, held, held_sems, tiles, sems, *refs = refs[:count], *refs[count:]
    half, height = start.shape

    def copies(t):
        k = jnp.maximum(ids[place + t], 0)
        yield pltpu.make_async_copy(right.at[k], held.at[t], held_sems.at[t])
        yield pltpu.make_async_copy(sources[t], tiles.at[t], sems.at[t])

    if not is_kept:
        blocks, sem = refs
        copy = pltpu.make_async_copy(theirs.at[half:, :LANES], blocks, sem)
        copy.start()
        copy.wait()
    for t in range(count):

        @pl.when(ids[place + t] >= 0)
        def _():
            for copy in copies(t):
                copy.start()

    out[:half, :] = start[...]
    for t in range(count):

        @pl.when(ids[place + t] >= 0)
        def _():
            for copy in copies(t):
                copy.wait()
            out[:half, :] += dot(held[t], second(tiles[t], 0))

    out[half:, :] = jnp.zeros((ROWS, height), jnp.float32)
    out[half:, :half] = in_row(check_sums(weights, out[:half, :]), 1)
    cube_term = spread(blocks[...], half, height) * out[:half, :]
    out[:half, :] = 3.0 * square[...] - 2.0 * cube_term if is_kept else -2.0 * cube_term


def diagonal_early_kernel(ids, *refs):
    lefts, out = refs[:-1], refs[-1]
    for j, left in enumerate(lefts):
        tile = left[: out.shape[0] // 2, :]
        term = dot(first(tile, 0), second(tile, 0), COLUMN_BY_COLUMN)
        out[...] = term if j == 0 else out[...] + term


def diagonal_kernel(ids, start, left, *refs):
    tiles, (given, kept, blocks, whole, held, sem) = refs[:-6], refs[-6:]
    half = given.shape[0]
    held[...] = jnp.zeros_like(held)
    for j, source in enumerate(tiles):

        @pl.when(ids[BACK] == j + 1)
        def _():
            copy = pltpu.make_async_copy(source.at[half:, :LANES], held, sem)
            copy.start()
            copy.wait()

    blocks[...] = held[...]
    tile = left[:half, :]
    whole[...] = start[...] + dot(first(tile, 0), second(tile, 0), COLUMN_BY_COLUMN)
    given[...] = whole[pl.ds(pl.multiple_of((1 - ids[CORE]) * half, half), half), :]
    kept[...] = whole[pl.ds(pl.multiple_of(ids[CORE] * half, half), half), :]


def early_kernel(ids, square, kept, received, blocks, kept_sum, received_sum, weights, *refs):
    rights, outs, (sums, held, sems) = refs[:2], refs[2:4], refs[4:]
    height = square.shape[1]
    fetch([right.at[place] for right in rights for place in (ids[COLUMN], ids[ROW])], held, sems)
    own = second(square[...], 0)
    diagonal = second((kept[...] + received[...]) * spread(blocks[...], *kept.shape), 0)
    for s, out in enumerate(outs):
        out[...] = dot(held[2 * s], own) + dot(held[2 * s + 1], diagonal)
    sums[...] = in_row(check_sums(weights, kept_sum[...] + received_sum[:, :height]), 0)


def in_steps(edges):
    sent, got, count = {}, {}, 0
    for source, target in edges:
        count = max(count, sum(e[0] == source for e in edges), sum(e[1] == target for e in edges))
    for source, target in edges:
        free = next(i for i in range(count) if (source, i) not in sent)
        other = next(i for i in range(count) if (target, i) not in got)
        if free != other:
            path, node, at_target, step = [], target, True, free
            while (node, step) in (got if at_target else sent):
                partner = (got if at_target else sent)[node, step]
                path.append((partner, node, step) if at_target else (node, partner, step))
                node, at_target, step = partner, not at_target, free + other - step
            for u, v, step in path:
                del sent[u, step], got[v, step]
            for u, v, step in path:
                sent[u, free + other - step], got[v, free + other - step] = v, u
        sent[source, free], got[target, free] = target, source
    return count, sent, got


def make_body(panels, columns):
    assert columns == 2 * panels and panels & (panels - 1) == 0
    chips = [(r, z) for r in range(panels) for z in range(panels)]

    edges = [((r, z), (z, z)) for r, z in chips if z != r]
    edges += [((r, z), (r, q)) for r, z in chips for q in range(panels) if z != r and q != r and q != z]
    steps, sent, got = in_steps(edges)
    down_step = [[-1] * panels for _ in range(panels)]
    tile_got = [[[-1] * steps for _ in range(panels)] for _ in range(panels)]
    for ((r, z), step), target in sent.items():
        if target[0] != r:
            down_step[r][z] = step
    for ((r, z), step), source in got.items():
        tile_got[r][z][step] = source[1] if source[0] == r else source[0]

    def send(value, target):
        pairs = []
        for r, z in chips:
            to = target(r, z)
            if to is not None:
                pairs += [(r * columns + 2 * z + core, to[0] * columns + 2 * to[1] + core) for core in (0, 1)]
        return lax.ppermute(value, ("row", "col"), pairs)

    def swap_core(value):
        return lax.ppermute(value, "col", [(c, c ^ 1) for c in range(columns)])

    def ring(step):
        return lambda r, z: (r, (z + step) % panels)

    def across(m):
        return lambda r, z: (r ^ m, z)

    def step_target(step, r, z):
        return sent.get(((r, z), step))

    powers = [1 << i for i in range(panels.bit_length() - 1)]

    def body(density, pattern, weights):
        r = lax.axis_index("row")
        c = lax.axis_index("col")
        z, core = c // 2, c % 2
        tile = density.T
        half, height = tile.shape

        scalars = [core, jnp.asarray(down_step)[r, z], r, z, (z - r) % panels]
        scalars += [r ^ m for m in range(panels)] + [(z - j) % panels for j in range(panels)]
        scalars += list(jnp.asarray(tile_got)[r, z])
        ids = jnp.stack([jnp.asarray(s, jnp.int32) for s in scalars])
        line_at, steps_at = LISTS + panels, LISTS + 2 * panels

        packed, mine, other, blocks = call(
            pack_kernel,
            [shape(half + ROWS, height), shape(half, half), shape(half + ROWS, half), shape(ROWS, LANES)],
            jnp.asarray(core, jnp.int32)[None],
            tile,
            pattern.T,
        )
        left = {0: packed, 1: send(packed, ring(1))}
        theirs = swap_core(other)
        own = jnp.concatenate([mine, theirs[:half]], axis=1)
        tiles = {m: send(own, across(m)) for m in powers}
        own_later = after(own, *[tiles[m] for m in powers])
        tiles = [own] + [tiles[m] if m in powers else send(own_later, across(m)) for m in range(1, panels)]
        last = panels // 2 + 1
        for j in range(2, last):
            left[j] = send(left[j - 1], ring(1))
        for j in range(panels - 1, last - 1, -1):
            left[j] = send(after(packed, own) if j == panels - 1 else left[j + 1], ring(-1))

        part = shape(panels, half, 3 * half, dtype=jnp.bfloat16)
        kept, given = call(split_kernel, [part] * 2, ids, *tiles)

        early = [j for j in range(panels) if j != last]
        starts = call(
            functools.partial(early_products_kernel, early, line_at),
            [shape(half, height)] * 2,
            ids,
            *[left[j] for j in early],
            kept,
            given,
            placed=2,
            scratch=held_parts(2 * len(early), half),
        )
        diagonal_start = call(diagonal_early_kernel, shape(height, height), ids, *[left[j] for j in early])
        kept_sum, given_sum = call(
            functools.partial(last_product_kernel, line_at + last),
            [shape(half, height), shape(half, height + half)],
            ids,
            left[last],
            after(starts[0], diagonal_start),
            starts[1],
            kept,
            given,
            placed=2,
            scratch=held_parts(2, half),
        )
        diagonal_given, diagonal_kept, diagonal_blocks = call(
            diagonal_kernel,
            [shape(half, height)] * 2 + [shape(ROWS, LANES)],
            ids,
            diagonal_start,
            left[last],
            *[left[j] for j in range(1, panels)],
            placed=panels - 1,
            scratch=[
                pltpu.VMEM((height, height), jnp.float32),
                pltpu.VMEM((ROWS, LANES), jnp.float32),
                pltpu.SemaphoreType.DMA,
            ],
        )
        received = swap_core(given_sum)
        square, *rows = call(
            square_kernel,
            [shape(half, height)] * (1 + steps),
            ids,
            after(kept_sum, diagonal_given),
            given_sum,
            received,
            blocks,
            theirs,
            placed=1,
            scratch=[pltpu.VMEM((ROWS, LANES), jnp.float32), pltpu.SemaphoreType.DMA],
        )

        arrived = [send(rows[step], functools.partial(step_target, step)) for step in range(steps)]
        *cube, sums = call(
            early_kernel,
            [shape(half, height)] * 2 + [shape(ROWS, half)],
            ids,
            square,
            diagonal_kept,
            swap_core(diagonal_given),
            diagonal_blocks,
            kept_sum,
            received,
            weights[None, :],
            kept,
            given,
            placed=2,
            scratch=held_parts(4, half),
        )

        held = [pltpu.VMEM((steps, half, height), jnp.float32), pltpu.SemaphoreType.DMA((steps,))]

        kernel = functools.partial(last_kernel, steps, steps_at)
        out = shape(half + ROWS, height)
        scratch = held_parts(steps, half) + held
        given_cube = call(
            functools.partial(kernel, False),
            out,
            ids,
            cube[1],
            weights[None, :],
            given,
            theirs,
            *arrived,
            placed=steps + 2,
            scratch=scratch + [pltpu.VMEM((ROWS, LANES), jnp.float32), pltpu.SemaphoreType.DMA],
        )
        kept_cube = call(
            functools.partial(kernel, True),
            out,
            ids,
            cube[0],
            weights[None, :],
            square,
            blocks,
            kept,
            *arrived,
            placed=steps + 1,
            scratch=scratch,
        )
        received = swap_core(given_cube)
        sums = sums + kept_cube[half:, :half] + received[half:, :half]
        sums = sums + sum(send(sums, across(m)) for m in range(1, panels))
        return (kept_cube[:half] + received[:half]).T, sums[:2]

    return body


def solution(mesh):
    in_specs = (P("row", "col"), P("row", "col"), P("row"))
    out_specs = (P("row", "col"), P(None, "col"))
    body = make_body(mesh.shape["row"], mesh.shape["col"])
    return jax.shard_map(body, mesh=mesh, in_specs=in_specs, out_specs=out_specs, check_vma=False)
```

```python
import functools

import jax
import jax.numpy as jnp
from jax import lax
from jax.experimental import pallas as pl
from jax.experimental.pallas import tpu as pltpu
from jax.sharding import PartitionSpec as P

BLK = 64
ROWS, LANES = 8, 128
VMEM_BYTES = 24 * 1024 * 1024
ROW_BY_COLUMN = ((1,), (0,))
ROW_BY_ROW = ((1,), (1,))
COLUMN_BY_COLUMN = ((0,), (0,))

CORE, DOWN, ROW, COLUMN, BACK, LISTS = range(6)


def parts(value):
    high = value.astype(jnp.bfloat16)
    return high, (value - high.astype(jnp.float32)).astype(jnp.bfloat16)


def first(value, axis):
    high, low = parts(value)
    return jnp.concatenate([high, high, low], axis=axis)


def second(value, axis):
    high, low = parts(value)
    return jnp.concatenate([high, low, high], axis=axis)


def dot(a, b, contract=ROW_BY_COLUMN):
    return lax.dot_general(a, b, (contract, ((), ())), preferred_element_type=jnp.float32)


def call(kernel, outs, ids, *arrays, placed=0, scratch=(), waits=False):
    pieces, held, homes = [], [], []
    for array in arrays[: len(arrays) - placed]:
        array = array if isinstance(array, list) else [array]
        rows = [a.shape[0] for a in array]
        homes += [(len(held), sum(rows[:i]), n, len(array) > 1) for i, n in enumerate(rows)]
        held.append(pltpu.VMEM((sum(rows), *array[0].shape[1:]), array[0].dtype))
        pieces += array
    arrays = pieces + list(arrays[len(arrays) - placed :])
    copied = len(pieces)
    n_outs = len(jax.tree.leaves(outs))

    def body(ids_ref, *refs):
        sources, rest, own = refs[:copied], refs[copied : len(arrays) + n_outs], refs[len(arrays) + n_outs :]
        targets, sems, own = own[: len(held)], own[len(held)], own[len(held) + 1 :]
        copies = []
        for i, (source, (home, start, n, part)) in enumerate(zip(sources, homes)):
            target = targets[home].at[start : start + n] if part else targets[home]
            copies.append(pltpu.make_async_copy(source, target, sems.at[i]))
        for copy in copies:
            copy.start()

        def arrive():
            for copy in copies:
                copy.wait()

        if waits:
            kernel(arrive, ids_ref, *targets, *rest, *own)
        else:
            arrive()
            kernel(ids_ref, *targets, *rest, *own)

    return pl.pallas_call(
        body,
        out_shape=outs,
        in_specs=[pl.BlockSpec(memory_space=pltpu.SMEM)] + [pl.BlockSpec(memory_space=pl.ANY)] * len(arrays),
        scratch_shapes=held + [pltpu.SemaphoreType.DMA((max(copied, 1),))] + list(scratch),
        compiler_params=pltpu.CompilerParams(vmem_limit_bytes=VMEM_BYTES),
    )(ids, *arrays)


def shape(*dims, dtype=jnp.float32):
    return jax.ShapeDtypeStruct(dims, dtype)


def after(value, *earlier):
    return lax.optimization_barrier((value, *earlier))[0]


def in_half(value, which):
    half = value.shape[1] // 2
    return jnp.where(which == 0, value[:, :half], value[:, half:])


def ones(count, wide, entry):
    dims = [wide, wide]
    dims[entry] = count * BLK
    entries = lax.broadcasted_iota(jnp.int32, dims, entry)
    return (lax.shift_right_logical(entries, BLK.bit_length() - 1) == lax.broadcasted_iota(jnp.int32, dims, 1 - entry)).astype(jnp.bfloat16)


def spread(blocks, half, height):
    wide = -(-height // BLK // 16) * 16
    rows = dot(ones(half // BLK, blocks.shape[0], 0), blocks[:, :wide].astype(jnp.bfloat16))
    return dot(rows.astype(jnp.bfloat16), ones(height // BLK, wide, 1))


def pack_kernel(core, tile, pattern, packed, mine, other, blocks):
    half, (wide, high) = tile.shape[0], pattern.shape
    packed[:half, :] = tile[...]
    packed[half:, :] = jnp.zeros((ROWS, tile.shape[1]), jnp.float32)

    def unit(rows, columns):
        same = lax.broadcasted_iota(jnp.int32, (rows, columns), 0) == lax.broadcasted_iota(jnp.int32, (rows, columns), 1)
        return same.astype(jnp.bfloat16)

    rows = dot(unit(ROWS, wide), pattern[...].astype(jnp.float32).astype(jnp.bfloat16))
    blocks[...] = dot(rows.astype(jnp.bfloat16), unit(high, LANES))
    packed[half:, :LANES] = blocks[...]
    mine[...] = in_half(tile[...], core[0])
    other[:half, :] = in_half(tile[...], 1 - core[0])
    other[half:, :] = jnp.zeros((ROWS, half), jnp.float32)
    other[half:, :LANES] = blocks[...]


def split_kernel(ids, *refs):
    tiles, (kept, given) = refs[:-2], refs[-2:]
    half = kept.shape[1]
    for m, tile in enumerate(tiles):
        kept[ids[LISTS + m]] = first(tile[:, :half], 1)
        given[ids[LISTS + m]] = first(tile[:, half:], 1)


def held_parts(count, half):
    return [pltpu.VMEM((count, half, 3 * half), jnp.bfloat16), pltpu.SemaphoreType.DMA((count,))]


def fetch(sources, held, sems, arrive=None):
    copies = [pltpu.make_async_copy(source, held.at[t], sems.at[t]) for t, source in enumerate(sources)]
    for copy in copies:
        copy.start()
    if arrive is not None:
        arrive()
    for copy in copies:
        copy.wait()


def sums_of_products(arrive, places, lefts, starts, rights, held, sems):
    half, count = held.shape[1], len(lefts)
    fetch([right.at[place] for right in rights for place in places], held, sems, arrive)
    totals = [None if start is None else start[...] for start in starts]
    for j, left in enumerate(lefts):
        value = second(left[:half, :], 0)
        for s in range(len(rights)):
            term = dot(held[s * count + j], value)
            totals[s] = term if totals[s] is None else totals[s] + term
    return totals


def early_products_kernel(early, line_at, arrive, ids, *refs):
    count = len(early)
    lefts, rights, outs, (held, sems) = refs[:count], refs[count : count + 2], refs[count + 2 : count + 4], refs[count + 4 :]
    places = [ids[line_at + j] for j in early]
    for out, total in zip(outs, sums_of_products(arrive, places, lefts, [None, None], rights, held, sems)):
        out[...] = total


def last_product_kernel(place, arrive, ids, left, start_kept, start_given, right_kept, right_given, kept, given, held, sems):
    height = kept.shape[1]
    starts = [start_kept, start_given]
    kept_sum, given_sum = sums_of_products(arrive, [ids[place]], [left], starts, [right_kept, right_given], held, sems)
    kept[...] = kept_sum
    given[:, :height] = given_sum
    given[:, height:] = in_half(kept_sum, 1 - ids[CORE])


def square_kernel(ids, kept, given, received, blocks, theirs, *refs):
    half, height = kept.shape
    square, outs, (their_blocks, sem) = refs[0], refs[1:-2], refs[-2:]
    copy = pltpu.make_async_copy(theirs.at[half:, :LANES], their_blocks, sem)
    copy.start()
    square[...] = (kept[...] + received[:, :height]) * spread(blocks[...], half, height)
    other = in_half(given[:, :height], ids[CORE]) + received[:, height:]
    copy.wait()
    other = (other * in_half(spread(their_blocks[...], half, height), ids[CORE])).T
    own = in_half(square[...], ids[CORE]).T
    for step, out in enumerate(outs):

        @pl.when(ids[DOWN] != step)
        def _():
            out[...] = square[...]

        @pl.when(ids[DOWN] == step)
        def _():
            out[:, :half] = jnp.where(ids[CORE] == 0, own, other)
            out[:, half:] = jnp.where(ids[CORE] == 0, other, own)


def check_sums(weights, value):
    column = jnp.sum(value * weights[...], axis=1, keepdims=True)
    return jnp.broadcast_to(column, (value.shape[0], LANES)).T[:ROWS, :]


def in_row(value, row):
    return jnp.where(lax.broadcasted_iota(jnp.int32, value.shape, 0) == row, value, 0.0)


def last_kernel(count, place, is_kept, arrive, ids, start, weights, *refs):
    if is_kept:
        square, blocks, *refs = refs
    right, *refs = refs
    if not is_kept:
        theirs, *refs = refs
    sources, out, held, held_sems, tiles, sems, *refs = refs[:count], *refs[count:]
    half, height = start.shape

    def copies(t):
        k = jnp.maximum(ids[place + t], 0)
        yield pltpu.make_async_copy(right.at[k], held.at[t], held_sems.at[t])
        yield pltpu.make_async_copy(sources[t], tiles.at[t], sems.at[t])

    if not is_kept:
        blocks, sem = refs
        blocks_copy = pltpu.make_async_copy(theirs.at[half:, :LANES], blocks, sem)
        blocks_copy.start()
    for t in range(count):

        @pl.when(ids[place + t] >= 0)
        def _():
            for copy in copies(t):
                copy.start()

    arrive()
    out[:half, :] = start[...]
    for t in range(count):

        @pl.when(ids[place + t] >= 0)
        def _():
            for copy in copies(t):
                copy.wait()
            out[:half, :] += dot(held[t], second(tiles[t], 0))

    out[half:, :] = jnp.zeros((ROWS, height), jnp.float32)
    out[half:, :half] = in_row(check_sums(weights, out[:half, :]), 1)
    if not is_kept:
        blocks_copy.wait()
    cube_term = spread(blocks[...], half, height) * out[:half, :]
    out[:half, :] = 3.0 * square[...] - 2.0 * cube_term if is_kept else -2.0 * cube_term


def diagonal_early_kernel(ids, *refs):
    lefts, out = refs[:-1], refs[-1]
    for j, left in enumerate(lefts):
        tile = left[: out.shape[0] // 2, :]
        term = dot(first(tile, 0), second(tile, 0), COLUMN_BY_COLUMN)
        out[...] = term if j == 0 else out[...] + term


def diagonal_kernel(ids, start, left, *refs):
    tiles, (given, kept, blocks, whole, held, sem) = refs[:-6], refs[-6:]
    half = given.shape[0]
    held[...] = jnp.zeros_like(held)
    for j, source in enumerate(tiles):

        @pl.when(ids[BACK] == j + 1)
        def _():
            copy = pltpu.make_async_copy(source.at[half:, :LANES], held, sem)
            copy.start()
            copy.wait()

    blocks[...] = held[...]
    tile = left[:half, :]
    whole[...] = start[...] + dot(first(tile, 0), second(tile, 0), COLUMN_BY_COLUMN)
    given[...] = whole[pl.ds(pl.multiple_of((1 - ids[CORE]) * half, half), half), :]
    kept[...] = whole[pl.ds(pl.multiple_of(ids[CORE] * half, half), half), :]


def early_kernel(ids, square, kept, received, blocks, kept_sum, received_sum, weights, *refs):
    rights, outs, (sums, held, sems) = refs[:2], refs[2:4], refs[4:]
    height = square.shape[1]
    fetch([right.at[place] for right in rights for place in (ids[COLUMN], ids[ROW])], held, sems)
    own = second(square[...], 0)
    diagonal = second((kept[...] + received[...]) * spread(blocks[...], *kept.shape), 0)
    for s, out in enumerate(outs):
        out[...] = dot(held[2 * s], own) + dot(held[2 * s + 1], diagonal)
    sums[...] = in_row(check_sums(weights, kept_sum[...] + received_sum[:, :height]), 0)


def in_steps(edges):
    sent, got, count = {}, {}, 0
    for source, target in edges:
        count = max(count, sum(e[0] == source for e in edges), sum(e[1] == target for e in edges))
    for source, target in edges:
        free = next(i for i in range(count) if (source, i) not in sent)
        other = next(i for i in range(count) if (target, i) not in got)
        if free != other:
            path, node, at_target, step = [], target, True, free
            while (node, step) in (got if at_target else sent):
                partner = (got if at_target else sent)[node, step]
                path.append((partner, node, step) if at_target else (node, partner, step))
                node, at_target, step = partner, not at_target, free + other - step
            for u, v, step in path:
                del sent[u, step], got[v, step]
            for u, v, step in path:
                sent[u, free + other - step], got[v, free + other - step] = v, u
        sent[source, free], got[target, free] = target, source
    return count, sent, got


def make_body(panels, columns):
    assert columns == 2 * panels and panels & (panels - 1) == 0
    chips = [(r, z) for r in range(panels) for z in range(panels)]

    edges = [((r, z), (z, z)) for r, z in chips if z != r]
    edges += [((r, z), (r, q)) for r, z in chips for q in range(panels) if z != r and q != r and q != z]
    steps, sent, got = in_steps(edges)
    down_step = [[-1] * panels for _ in range(panels)]
    tile_got = [[[-1] * steps for _ in range(panels)] for _ in range(panels)]
    for ((r, z), step), target in sent.items():
        if target[0] != r:
            down_step[r][z] = step
    for ((r, z), step), source in got.items():
        tile_got[r][z][step] = source[1] if source[0] == r else source[0]

    def send(value, target):
        pairs = []
        for r, z in chips:
            to = target(r, z)
            if to is not None:
                pairs += [(r * columns + 2 * z + core, to[0] * columns + 2 * to[1] + core) for core in (0, 1)]
        return lax.ppermute(value, ("row", "col"), pairs)

    def swap_core(value):
        return lax.ppermute(value, "col", [(c, c ^ 1) for c in range(columns)])

    def ring(step):
        return lambda r, z: (r, (z + step) % panels)

    def across(m):
        return lambda r, z: (r ^ m, z)

    def step_target(step, r, z):
        return sent.get(((r, z), step))

    powers = [1 << i for i in range(panels.bit_length() - 1)]

    def body(density, pattern, weights):
        r = lax.axis_index("row")
        c = lax.axis_index("col")
        z, core = c // 2, c % 2
        tile = density.T
        half, height = tile.shape

        scalars = [core, jnp.asarray(down_step)[r, z], r, z, (z - r) % panels]
        scalars += [r ^ m for m in range(panels)] + [(z - j) % panels for j in range(panels)]
        scalars += list(jnp.asarray(tile_got)[r, z])
        ids = jnp.stack([jnp.asarray(s, jnp.int32) for s in scalars])
        line_at, steps_at = LISTS + panels, LISTS + 2 * panels

        packed, mine, other, blocks = call(
            pack_kernel,
            [shape(half + ROWS, height), shape(half, half), shape(half + ROWS, half), shape(ROWS, LANES)],
            jnp.asarray(core, jnp.int32)[None],
            tile,
            pattern.T,
        )
        left = {0: packed, 1: send(packed, ring(1))}
        theirs = swap_core(other)
        own = jnp.concatenate([mine, theirs[:half]], axis=1)
        tiles = {m: send(own, across(m)) for m in powers}
        own_later = after(own, *[tiles[m] for m in powers])
        tiles = [own] + [tiles[m] if m in powers else send(own_later, across(m)) for m in range(1, panels)]
        last = panels // 2 + 1
        for j in range(2, last):
            left[j] = send(left[j - 1], ring(1))
        for j in range(panels - 1, last - 1, -1):
            left[j] = send(after(packed, own) if j == panels - 1 else left[j + 1], ring(-1))

        part = shape(panels, half, 3 * half, dtype=jnp.bfloat16)
        kept, given = call(split_kernel, [part] * 2, ids, *tiles)

        early = [j for j in range(panels) if j != last]
        starts = call(
            functools.partial(early_products_kernel, early, line_at),
            [shape(half, height)] * 2,
            ids,
            *[left[j] for j in early],
            kept,
            given,
            placed=2,
            scratch=held_parts(2 * len(early), half),
            waits=True,
        )
        diagonal_start = call(diagonal_early_kernel, shape(height, height), ids, *[left[j] for j in early])
        kept_sum, given_sum = call(
            functools.partial(last_product_kernel, line_at + last),
            [shape(half, height), shape(half, height + half)],
            ids,
            left[last],
            after(starts[0], diagonal_start),
            starts[1],
            kept,
            given,
            placed=2,
            scratch=held_parts(2, half),
            waits=True,
        )
        diagonal_given, diagonal_kept, diagonal_blocks = call(
            diagonal_kernel,
            [shape(half, height)] * 2 + [shape(ROWS, LANES)],
            ids,
            diagonal_start,
            left[last],
            *[left[j] for j in range(1, panels)],
            placed=panels - 1,
            scratch=[
                pltpu.VMEM((height, height), jnp.float32),
                pltpu.VMEM((ROWS, LANES), jnp.float32),
                pltpu.SemaphoreType.DMA,
            ],
        )
        received = swap_core(given_sum)
        square, *rows = call(
            square_kernel,
            [shape(half, height)] * (1 + steps),
            ids,
            after(kept_sum, diagonal_given),
            given_sum,
            received,
            blocks,
            theirs,
            placed=1,
            scratch=[pltpu.VMEM((ROWS, LANES), jnp.float32), pltpu.SemaphoreType.DMA],
        )

        arrived = [send(rows[step], functools.partial(step_target, step)) for step in range(steps)]
        *cube, sums = call(
            early_kernel,
            [shape(half, height)] * 2 + [shape(ROWS, half)],
            ids,
            square,
            diagonal_kept,
            swap_core(diagonal_given),
            diagonal_blocks,
            kept_sum,
            received,
            weights[None, :],
            kept,
            given,
            placed=2,
            scratch=held_parts(4, half),
        )

        held = [pltpu.VMEM((steps, half, height), jnp.float32), pltpu.SemaphoreType.DMA((steps,))]

        kernel = functools.partial(last_kernel, steps, steps_at)
        out = shape(half + ROWS, height)
        scratch = held_parts(steps, half) + held
        given_cube = call(
            functools.partial(kernel, False),
            out,
            ids,
            cube[1],
            weights[None, :],
            given,
            theirs,
            *arrived,
            placed=steps + 2,
            waits=True,
            scratch=scratch + [pltpu.VMEM((ROWS, LANES), jnp.float32), pltpu.SemaphoreType.DMA],
        )
        kept_cube = call(
            functools.partial(kernel, True),
            out,
            ids,
            cube[0],
            weights[None, :],
            square,
            blocks,
            kept,
            *arrived,
            placed=steps + 1,
            waits=True,
            scratch=scratch,
        )
        received = swap_core(given_cube)
        sums = sums + kept_cube[half:, :half] + received[half:, :half]
        sums = sums + sum(send(sums, across(m)) for m in range(1, panels))
        return (kept_cube[:half] + received[:half]).T, sums[:2]

    return body


def solution(mesh):
    in_specs = (P("row", "col"), P("row", "col"), P("row"))
    out_specs = (P("row", "col"), P(None, "col"))
    body = make_body(mesh.shape["row"], mesh.shape["col"])
    return jax.shard_map(body, mesh=mesh, in_specs=in_specs, out_specs=out_specs, check_vma=False)
```

```python
import functools

import jax
import jax.numpy as jnp
from jax import lax
from jax.experimental import pallas as pl
from jax.experimental.pallas import tpu as pltpu
from jax.sharding import PartitionSpec as P

BLK = 64
ROWS, LANES = 8, 128
VMEM_BYTES = 24 * 1024 * 1024
ROW_BY_COLUMN = ((1,), (0,))
ROW_BY_ROW = ((1,), (1,))
COLUMN_BY_COLUMN = ((0,), (0,))

CORE, DOWN, ROW, COLUMN, BACK, LISTS = range(6)


def parts(value):
    high = value.astype(jnp.bfloat16)
    return high, (value - high.astype(jnp.float32)).astype(jnp.bfloat16)


def first(value, axis):
    high, low = parts(value)
    return jnp.concatenate([high, high, low], axis=axis)


def second(value, axis):
    high, low = parts(value)
    return jnp.concatenate([high, low, high], axis=axis)


def dot(a, b, contract=ROW_BY_COLUMN):
    return lax.dot_general(a, b, (contract, ((), ())), preferred_element_type=jnp.float32)


def call(kernel, outs, ids, *arrays, placed=0, scratch=(), waits=False):
    pieces, held, homes = [], [], []
    for array in arrays[: len(arrays) - placed]:
        array = array if isinstance(array, list) else [array]
        rows = [a.shape[0] for a in array]
        homes += [(len(held), sum(rows[:i]), n, len(array) > 1) for i, n in enumerate(rows)]
        held.append(pltpu.VMEM((sum(rows), *array[0].shape[1:]), array[0].dtype))
        pieces += array
    arrays = pieces + list(arrays[len(arrays) - placed :])
    copied = len(pieces)
    n_outs = len(jax.tree.leaves(outs))

    def body(ids_ref, *refs):
        sources, rest, own = refs[:copied], refs[copied : len(arrays) + n_outs], refs[len(arrays) + n_outs :]
        targets, sems, own = own[: len(held)], own[len(held)], own[len(held) + 1 :]
        copies = []
        for i, (source, (home, start, n, part)) in enumerate(zip(sources, homes)):
            target = targets[home].at[start : start + n] if part else targets[home]
            copies.append(pltpu.make_async_copy(source, target, sems.at[i]))
        for copy in copies:
            copy.start()

        def arrive():
            for copy in copies:
                copy.wait()

        if waits:
            kernel(arrive, ids_ref, *targets, *rest, *own)
        else:
            arrive()
            kernel(ids_ref, *targets, *rest, *own)

    return pl.pallas_call(
        body,
        out_shape=outs,
        in_specs=[pl.BlockSpec(memory_space=pltpu.SMEM)] + [pl.BlockSpec(memory_space=pl.ANY)] * len(arrays),
        scratch_shapes=held + [pltpu.SemaphoreType.DMA((max(copied, 1),))] + list(scratch),
        compiler_params=pltpu.CompilerParams(vmem_limit_bytes=VMEM_BYTES),
    )(ids, *arrays)


def shape(*dims, dtype=jnp.float32):
    return jax.ShapeDtypeStruct(dims, dtype)


def after(value, *earlier):
    return lax.optimization_barrier((value, *earlier))[0]


def in_half(value, which):
    half = value.shape[1] // 2
    return jnp.where(which == 0, value[:, :half], value[:, half:])


def ones(count, wide, entry):
    dims = [wide, wide]
    dims[entry] = count * BLK
    entries = lax.broadcasted_iota(jnp.int32, dims, entry)
    return (lax.shift_right_logical(entries, BLK.bit_length() - 1) == lax.broadcasted_iota(jnp.int32, dims, 1 - entry)).astype(jnp.bfloat16)


def spread(blocks, half, height):
    wide = -(-height // BLK // 16) * 16
    rows = dot(ones(half // BLK, blocks.shape[0], 0), blocks[:, :wide].astype(jnp.bfloat16))
    return dot(rows.astype(jnp.bfloat16), ones(height // BLK, wide, 1))


def pack_kernel(core, tile, pattern, packed, mine, other, blocks):
    half, (wide, high) = tile.shape[0], pattern.shape
    packed[:half, :] = tile[...]
    packed[half:, :] = jnp.zeros((ROWS, tile.shape[1]), jnp.float32)

    def unit(rows, columns):
        same = lax.broadcasted_iota(jnp.int32, (rows, columns), 0) == lax.broadcasted_iota(jnp.int32, (rows, columns), 1)
        return same.astype(jnp.bfloat16)

    rows = dot(unit(ROWS, wide), pattern[...].astype(jnp.float32).astype(jnp.bfloat16))
    blocks[...] = dot(rows.astype(jnp.bfloat16), unit(high, LANES))
    packed[half:, :LANES] = blocks[...]
    mine[...] = in_half(tile[...], core[0])
    other[:half, :] = in_half(tile[...], 1 - core[0])
    other[half:, :] = jnp.zeros((ROWS, half), jnp.float32)
    other[half:, :LANES] = blocks[...]


def split_kernel(ids, *refs):
    tiles, (kept, given) = refs[:-2], refs[-2:]
    half = kept.shape[1]
    for m, tile in enumerate(tiles):
        kept[ids[LISTS + m]] = first(tile[:, :half], 1)
        given[ids[LISTS + m]] = first(tile[:, half:], 1)


def held_parts(count, half):
    return [pltpu.VMEM((count, half, 3 * half), jnp.bfloat16), pltpu.SemaphoreType.DMA((count,))]


def fetch(sources, held, sems, arrive=None):
    copies = [pltpu.make_async_copy(source, held.at[t], sems.at[t]) for t, source in enumerate(sources)]
    for copy in copies:
        copy.start()
    if arrive is not None:
        arrive()
    for copy in copies:
        copy.wait()


def sums_of_products(arrive, places, lefts, starts, rights, held, sems):
    half, count = held.shape[1], len(lefts)
    fetch([right.at[place] for right in rights for place in places], held, sems, arrive)
    totals = [None if start is None else start[...] for start in starts]
    for j, left in enumerate(lefts):
        value = second(left[:half, :], 0)
        for s in range(len(rights)):
            term = dot(held[s * count + j], value)
            totals[s] = term if totals[s] is None else totals[s] + term
    return totals


def early_products_kernel(early, line_at, arrive, ids, *refs):
    count = len(early)
    lefts, rights, outs, (held, sems) = refs[:count], refs[count : count + 2], refs[count + 2 : count + 4], refs[count + 4 :]
    places = [ids[line_at + j] for j in early]
    for out, total in zip(outs, sums_of_products(arrive, places, lefts, [None, None], rights, held, sems)):
        out[...] = total


def last_product_kernel(place, arrive, ids, left, start_kept, start_given, right_kept, right_given, kept, given, held, sems):
    height = kept.shape[1]
    starts = [start_kept, start_given]
    kept_sum, given_sum = sums_of_products(arrive, [ids[place]], [left], starts, [right_kept, right_given], held, sems)
    kept[...] = kept_sum
    given[:, :height] = given_sum
    given[:, height:] = in_half(kept_sum, 1 - ids[CORE])


def square_kernel(ids, kept, given, received, blocks, theirs, *refs):
    half, height = kept.shape
    square, outs, (their_blocks, sem) = refs[0], refs[1:-2], refs[-2:]
    copy = pltpu.make_async_copy(theirs.at[half:, :LANES], their_blocks, sem)
    copy.start()
    square[...] = (kept[...] + received[:, :height]) * spread(blocks[...], half, height)
    other = in_half(given[:, :height], ids[CORE]) + received[:, height:]
    copy.wait()
    other = (other * in_half(spread(their_blocks[...], half, height), ids[CORE])).T
    own = in_half(square[...], ids[CORE]).T
    for step, out in enumerate(outs):

        @pl.when(ids[DOWN] != step)
        def _():
            out[...] = square[...]

        @pl.when(ids[DOWN] == step)
        def _():
            out[:, :half] = jnp.where(ids[CORE] == 0, own, other)
            out[:, half:] = jnp.where(ids[CORE] == 0, other, own)


def check_sums(weights, value):
    column = jnp.sum(value * weights[...], axis=1, keepdims=True)
    return jnp.broadcast_to(column, (value.shape[0], LANES)).T[:ROWS, :]


def in_row(value, row):
    return jnp.where(lax.broadcasted_iota(jnp.int32, value.shape, 0) == row, value, 0.0)


def middle_kernel(place, ids, tile, *refs):
    starts, rights, outs, (held, sems) = refs[:2], refs[2:4], refs[4:6], refs[6:]
    k = ids[place]
    fetch([right.at[jnp.maximum(k, 0)] for right in rights], held, sems)

    @pl.when(k >= 0)
    def _():
        value = second(tile[...], 0)
        for s, (out, start) in enumerate(zip(outs, starts)):
            out[...] = start[...] + dot(held[s], value)

    @pl.when(k < 0)
    def _():
        for out, start in zip(outs, starts):
            out[...] = start[...]


def last_kernel(count, place, is_kept, arrive, ids, start, weights, *refs):
    if is_kept:
        square, blocks, *refs = refs
    right, *refs = refs
    if not is_kept:
        theirs, *refs = refs
    sources, out, held, held_sems, tiles, sems, *refs = refs[:count], *refs[count:]
    half, height = start.shape

    def copies(t):
        k = jnp.maximum(ids[place + t], 0)
        yield pltpu.make_async_copy(right.at[k], held.at[t], held_sems.at[t])
        yield pltpu.make_async_copy(sources[t], tiles.at[t], sems.at[t])

    if not is_kept:
        blocks, sem = refs
        blocks_copy = pltpu.make_async_copy(theirs.at[half:, :LANES], blocks, sem)
        blocks_copy.start()
    for t in range(count):

        @pl.when(ids[place + t] >= 0)
        def _():
            for copy in copies(t):
                copy.start()

    arrive()
    out[:half, :] = start[...]
    for t in range(count):

        @pl.when(ids[place + t] >= 0)
        def _():
            for copy in copies(t):
                copy.wait()
            out[:half, :] += dot(held[t], second(tiles[t], 0))

    out[half:, :] = jnp.zeros((ROWS, height), jnp.float32)
    out[half:, :half] = in_row(check_sums(weights, out[:half, :]), 1)
    if not is_kept:
        blocks_copy.wait()
    cube_term = spread(blocks[...], half, height) * out[:half, :]
    out[:half, :] = 3.0 * square[...] - 2.0 * cube_term if is_kept else -2.0 * cube_term


def diagonal_early_kernel(ids, *refs):
    lefts, out = refs[:-1], refs[-1]
    for j, left in enumerate(lefts):
        tile = left[: out.shape[0] // 2, :]
        term = dot(first(tile, 0), second(tile, 0), COLUMN_BY_COLUMN)
        out[...] = term if j == 0 else out[...] + term


def diagonal_kernel(ids, start, left, *refs):
    tiles, (given, kept, blocks, whole, held, sem) = refs[:-6], refs[-6:]
    half = given.shape[0]
    held[...] = jnp.zeros_like(held)
    for j, source in enumerate(tiles):

        @pl.when(ids[BACK] == j + 1)
        def _():
            copy = pltpu.make_async_copy(source.at[half:, :LANES], held, sem)
            copy.start()
            copy.wait()

    blocks[...] = held[...]
    tile = left[:half, :]
    whole[...] = start[...] + dot(first(tile, 0), second(tile, 0), COLUMN_BY_COLUMN)
    given[...] = whole[pl.ds(pl.multiple_of((1 - ids[CORE]) * half, half), half), :]
    kept[...] = whole[pl.ds(pl.multiple_of(ids[CORE] * half, half), half), :]


def early_kernel(ids, square, kept, received, blocks, kept_sum, received_sum, weights, *refs):
    rights, outs, (sums, held, sems) = refs[:2], refs[2:4], refs[4:]
    height = square.shape[1]
    fetch([right.at[place] for right in rights for place in (ids[COLUMN], ids[ROW])], held, sems)
    own = second(square[...], 0)
    diagonal = second((kept[...] + received[...]) * spread(blocks[...], *kept.shape), 0)
    for s, out in enumerate(outs):
        out[...] = dot(held[2 * s], own) + dot(held[2 * s + 1], diagonal)
    sums[...] = in_row(check_sums(weights, kept_sum[...] + received_sum[:, :height]), 0)


def in_steps(edges):
    sent, got, count = {}, {}, 0
    for source, target in edges:
        count = max(count, sum(e[0] == source for e in edges), sum(e[1] == target for e in edges))
    for source, target in edges:
        free = next(i for i in range(count) if (source, i) not in sent)
        other = next(i for i in range(count) if (target, i) not in got)
        if free != other:
            path, node, at_target, step = [], target, True, free
            while (node, step) in (got if at_target else sent):
                partner = (got if at_target else sent)[node, step]
                path.append((partner, node, step) if at_target else (node, partner, step))
                node, at_target, step = partner, not at_target, free + other - step
            for u, v, step in path:
                del sent[u, step], got[v, step]
            for u, v, step in path:
                sent[u, free + other - step], got[v, free + other - step] = v, u
        sent[source, free], got[target, free] = target, source
    return count, sent, got


def make_body(panels, columns):
    assert columns == 2 * panels and panels & (panels - 1) == 0
    chips = [(r, z) for r in range(panels) for z in range(panels)]

    edges = [((r, z), (z, z)) for r, z in chips if z != r]
    edges += [((r, z), (r, q)) for r, z in chips for q in range(panels) if z != r and q != r and q != z]
    steps, sent, got = in_steps(edges)
    down_step = [[-1] * panels for _ in range(panels)]
    tile_got = [[[-1] * steps for _ in range(panels)] for _ in range(panels)]
    for ((r, z), step), target in sent.items():
        if target[0] != r:
            down_step[r][z] = step
    for ((r, z), step), source in got.items():
        tile_got[r][z][step] = source[1] if source[0] == r else source[0]

    def send(value, target):
        pairs = []
        for r, z in chips:
            to = target(r, z)
            if to is not None:
                pairs += [(r * columns + 2 * z + core, to[0] * columns + 2 * to[1] + core) for core in (0, 1)]
        return lax.ppermute(value, ("row", "col"), pairs)

    def swap_core(value):
        return lax.ppermute(value, "col", [(c, c ^ 1) for c in range(columns)])

    def ring(step):
        return lambda r, z: (r, (z + step) % panels)

    def across(m):
        return lambda r, z: (r ^ m, z)

    def step_target(step, r, z):
        return sent.get(((r, z), step))

    powers = [1 << i for i in range(panels.bit_length() - 1)]

    def body(density, pattern, weights):
        r = lax.axis_index("row")
        c = lax.axis_index("col")
        z, core = c // 2, c % 2
        tile = density.T
        half, height = tile.shape

        scalars = [core, jnp.asarray(down_step)[r, z], r, z, (z - r) % panels]
        scalars += [r ^ m for m in range(panels)] + [(z - j) % panels for j in range(panels)]
        scalars += list(jnp.asarray(tile_got)[r, z])
        ids = jnp.stack([jnp.asarray(s, jnp.int32) for s in scalars])
        line_at, steps_at = LISTS + panels, LISTS + 2 * panels

        packed, mine, other, blocks = call(
            pack_kernel,
            [shape(half + ROWS, height), shape(half, half), shape(half + ROWS, half), shape(ROWS, LANES)],
            jnp.asarray(core, jnp.int32)[None],
            tile,
            pattern.T,
        )
        left = {0: packed, 1: send(packed, ring(1))}
        theirs = swap_core(other)
        own = jnp.concatenate([mine, theirs[:half]], axis=1)
        tiles = {m: send(own, across(m)) for m in powers}
        own_later = after(own, *[tiles[m] for m in powers])
        tiles = [own] + [tiles[m] if m in powers else send(own_later, across(m)) for m in range(1, panels)]
        last = panels // 2 + 1
        for j in range(2, last):
            left[j] = send(left[j - 1], ring(1))
        for j in range(panels - 1, last - 1, -1):
            left[j] = send(after(packed, own) if j == panels - 1 else left[j + 1], ring(-1))

        part = shape(panels, half, 3 * half, dtype=jnp.bfloat16)
        kept, given = call(split_kernel, [part] * 2, ids, *tiles)

        early = [j for j in range(panels) if j != last]
        starts = call(
            functools.partial(early_products_kernel, early, line_at),
            [shape(half, height)] * 2,
            ids,
            *[left[j] for j in early],
            kept,
            given,
            placed=2,
            scratch=held_parts(2 * len(early), half),
            waits=True,
        )
        diagonal_start = call(diagonal_early_kernel, shape(height, height), ids, *[left[j] for j in early])
        kept_sum, given_sum = call(
            functools.partial(last_product_kernel, line_at + last),
            [shape(half, height), shape(half, height + half)],
            ids,
            left[last],
            after(starts[0], diagonal_start),
            starts[1],
            kept,
            given,
            placed=2,
            scratch=held_parts(2, half),
            waits=True,
        )
        diagonal_given, diagonal_kept, diagonal_blocks = call(
            diagonal_kernel,
            [shape(half, height)] * 2 + [shape(ROWS, LANES)],
            ids,
            diagonal_start,
            left[last],
            *[left[j] for j in range(1, panels)],
            placed=panels - 1,
            scratch=[
                pltpu.VMEM((height, height), jnp.float32),
                pltpu.VMEM((ROWS, LANES), jnp.float32),
                pltpu.SemaphoreType.DMA,
            ],
        )
        received = swap_core(given_sum)
        square, *rows = call(
            square_kernel,
            [shape(half, height)] * (1 + steps),
            ids,
            after(kept_sum, diagonal_given),
            given_sum,
            received,
            blocks,
            theirs,
            placed=1,
            scratch=[pltpu.VMEM((ROWS, LANES), jnp.float32), pltpu.SemaphoreType.DMA],
        )

        arrived = [send(rows[step], functools.partial(step_target, step)) for step in range(steps)]
        *cube, sums = call(
            early_kernel,
            [shape(half, height)] * 2 + [shape(ROWS, half)],
            ids,
            square,
            diagonal_kept,
            swap_core(diagonal_given),
            diagonal_blocks,
            kept_sum,
            received,
            weights[None, :],
            kept,
            given,
            placed=2,
            scratch=held_parts(4, half),
        )

        cube = call(
            functools.partial(middle_kernel, steps_at),
            [shape(half, height)] * 2,
            ids,
            arrived[0],
            *cube,
            kept,
            given,
            placed=2,
            scratch=held_parts(2, half),
        )
        steps_at, steps_left, arrived = steps_at + 1, steps - 1, arrived[1:]
        held = [pltpu.VMEM((steps_left, half, height), jnp.float32), pltpu.SemaphoreType.DMA((steps_left,))]

        kernel = functools.partial(last_kernel, steps_left, steps_at)
        out = shape(half + ROWS, height)
        scratch = held_parts(steps_left, half) + held
        given_cube = call(
            functools.partial(kernel, False),
            out,
            ids,
            cube[1],
            weights[None, :],
            given,
            theirs,
            *arrived,
            placed=steps_left + 2,
            waits=True,
            scratch=scratch + [pltpu.VMEM((ROWS, LANES), jnp.float32), pltpu.SemaphoreType.DMA],
        )
        kept_cube = call(
            functools.partial(kernel, True),
            out,
            ids,
            cube[0],
            weights[None, :],
            square,
            blocks,
            kept,
            *arrived,
            placed=steps_left + 1,
            waits=True,
            scratch=scratch,
        )
        received = swap_core(given_cube)
        sums = sums + kept_cube[half:, :half] + received[half:, :half]
        sums = sums + sum(send(sums, across(m)) for m in range(1, panels))
        return (kept_cube[:half] + received[:half]).T, sums[:2]

    return body


def solution(mesh):
    in_specs = (P("row", "col"), P("row", "col"), P("row"))
    out_specs = (P("row", "col"), P(None, "col"))
    body = make_body(mesh.shape["row"], mesh.shape["col"])
    return jax.shard_map(body, mesh=mesh, in_specs=in_specs, out_specs=out_specs, check_vma=False)
```

```python
import functools

import jax
import jax.numpy as jnp
from jax import lax
from jax.experimental import pallas as pl
from jax.experimental.pallas import tpu as pltpu
from jax.sharding import PartitionSpec as P

BLK = 64
ROWS, LANES = 8, 128
VMEM_BYTES = 24 * 1024 * 1024
ROW_BY_COLUMN = ((1,), (0,))
ROW_BY_ROW = ((1,), (1,))
COLUMN_BY_COLUMN = ((0,), (0,))

CORE, DOWN, ROW, COLUMN, BACK, LISTS = range(6)


def parts(value):
    high = value.astype(jnp.bfloat16)
    return high, (value - high.astype(jnp.float32)).astype(jnp.bfloat16)


def first(value, axis):
    high, low = parts(value)
    return jnp.concatenate([high, high, low], axis=axis)


def second(value, axis):
    high, low = parts(value)
    return jnp.concatenate([high, low, high], axis=axis)


def dot(a, b, contract=ROW_BY_COLUMN):
    return lax.dot_general(a, b, (contract, ((), ())), preferred_element_type=jnp.float32)


def call(kernel, outs, ids, *arrays, placed=0, scratch=(), waits=False):
    pieces, held, homes = [], [], []
    for array in arrays[: len(arrays) - placed]:
        array = array if isinstance(array, list) else [array]
        rows = [a.shape[0] for a in array]
        homes += [(len(held), sum(rows[:i]), n, len(array) > 1) for i, n in enumerate(rows)]
        held.append(pltpu.VMEM((sum(rows), *array[0].shape[1:]), array[0].dtype))
        pieces += array
    arrays = pieces + list(arrays[len(arrays) - placed :])
    copied = len(pieces)
    n_outs = len(jax.tree.leaves(outs))

    def body(ids_ref, *refs):
        sources, rest, own = refs[:copied], refs[copied : len(arrays) + n_outs], refs[len(arrays) + n_outs :]
        targets, sems, own = own[: len(held)], own[len(held)], own[len(held) + 1 :]
        copies = []
        for i, (source, (home, start, n, part)) in enumerate(zip(sources, homes)):
            target = targets[home].at[start : start + n] if part else targets[home]
            copies.append(pltpu.make_async_copy(source, target, sems.at[i]))
        for copy in copies:
            copy.start()

        def arrive():
            for copy in copies:
                copy.wait()

        if waits:
            kernel(arrive, ids_ref, *targets, *rest, *own)
        else:
            arrive()
            kernel(ids_ref, *targets, *rest, *own)

    return pl.pallas_call(
        body,
        out_shape=outs,
        in_specs=[pl.BlockSpec(memory_space=pltpu.SMEM)] + [pl.BlockSpec(memory_space=pl.ANY)] * len(arrays),
        scratch_shapes=held + [pltpu.SemaphoreType.DMA((max(copied, 1),))] + list(scratch),
        compiler_params=pltpu.CompilerParams(vmem_limit_bytes=VMEM_BYTES),
    )(ids, *arrays)


def shape(*dims, dtype=jnp.float32):
    return jax.ShapeDtypeStruct(dims, dtype)


def after(value, *earlier):
    return lax.optimization_barrier((value, *earlier))[0]


def in_half(value, which):
    half = value.shape[1] // 2
    return jnp.where(which == 0, value[:, :half], value[:, half:])


def ones(count, wide, entry):
    dims = [wide, wide]
    dims[entry] = count * BLK
    entries = lax.broadcasted_iota(jnp.int32, dims, entry)
    return (lax.shift_right_logical(entries, BLK.bit_length() - 1) == lax.broadcasted_iota(jnp.int32, dims, 1 - entry)).astype(jnp.bfloat16)


def spread(blocks, half, height):
    wide = -(-height // BLK // 16) * 16
    rows = dot(ones(half // BLK, blocks.shape[0], 0), blocks[:, :wide].astype(jnp.bfloat16))
    return dot(rows.astype(jnp.bfloat16), ones(height // BLK, wide, 1))


def pack_kernel(core, tile, pattern, packed, mine, other, blocks):
    half, (wide, high) = tile.shape[0], pattern.shape
    packed[:half, :] = tile[...]
    packed[half:, :] = jnp.zeros((ROWS, tile.shape[1]), jnp.float32)

    def unit(rows, columns):
        same = lax.broadcasted_iota(jnp.int32, (rows, columns), 0) == lax.broadcasted_iota(jnp.int32, (rows, columns), 1)
        return same.astype(jnp.bfloat16)

    rows = dot(unit(ROWS, wide), pattern[...].astype(jnp.float32).astype(jnp.bfloat16))
    blocks[...] = dot(rows.astype(jnp.bfloat16), unit(high, LANES))
    packed[half:, :LANES] = blocks[...]
    mine[...] = in_half(tile[...], core[0])
    other[:half, :] = in_half(tile[...], 1 - core[0])
    other[half:, :] = jnp.zeros((ROWS, half), jnp.float32)
    other[half:, :LANES] = blocks[...]


def split_kernel(ids, *refs):
    tiles, (kept, given) = refs[:-2], refs[-2:]
    half = kept.shape[1]
    for m, tile in enumerate(tiles):
        kept[ids[LISTS + m]] = first(tile[:, :half], 1)
        given[ids[LISTS + m]] = first(tile[:, half:], 1)


def held_parts(count, half):
    return [pltpu.VMEM((count, half, 3 * half), jnp.bfloat16), pltpu.SemaphoreType.DMA((count,))]


def fetch(sources, held, sems, arrive=None):
    copies = [pltpu.make_async_copy(source, held.at[t], sems.at[t]) for t, source in enumerate(sources)]
    for copy in copies:
        copy.start()
    if arrive is not None:
        arrive()
    for copy in copies:
        copy.wait()


def sums_of_products(arrive, places, lefts, starts, rights, held, sems):
    half, count = held.shape[1], len(lefts)
    fetch([right.at[place] for right in rights for place in places], held, sems, arrive)
    totals = [None if start is None else start[...] for start in starts]
    for j, left in enumerate(lefts):
        value = second(left[:half, :], 0)
        for s in range(len(rights)):
            term = dot(held[s * count + j], value)
            totals[s] = term if totals[s] is None else totals[s] + term
    return totals


def early_products_kernel(early, line_at, arrive, ids, *refs):
    count = len(early)
    lefts, rights, outs, (held, sems) = refs[:count], refs[count : count + 2], refs[count + 2 : count + 4], refs[count + 4 :]
    places = [ids[line_at + j] for j in early]
    for out, total in zip(outs, sums_of_products(arrive, places, lefts, [None, None], rights, held, sems)):
        out[...] = total


def last_product_kernel(place, arrive, ids, left, start_kept, start_given, right_kept, right_given, kept, given, held, sems):
    height = kept.shape[1]
    starts = [start_kept, start_given]
    kept_sum, given_sum = sums_of_products(arrive, [ids[place]], [left], starts, [right_kept, right_given], held, sems)
    kept[...] = kept_sum
    given[:, :height] = given_sum
    given[:, height:] = in_half(kept_sum, 1 - ids[CORE])


def square_kernel(ids, kept, given, received, blocks, theirs, *refs):
    half, height = kept.shape
    square, outs, (their_blocks, sem) = refs[0], refs[1:-2], refs[-2:]
    copy = pltpu.make_async_copy(theirs.at[half:, :LANES], their_blocks, sem)
    copy.start()
    square[...] = (kept[...] + received[:, :height]) * spread(blocks[...], half, height)
    other = in_half(given[:, :height], ids[CORE]) + received[:, height:]
    copy.wait()
    other = (other * in_half(spread(their_blocks[...], half, height), ids[CORE])).T
    own = in_half(square[...], ids[CORE]).T
    for step, out in enumerate(outs):

        @pl.when(ids[DOWN] != step)
        def _():
            out[...] = square[...]

        @pl.when(ids[DOWN] == step)
        def _():
            out[:, :half] = jnp.where(ids[CORE] == 0, own, other)
            out[:, half:] = jnp.where(ids[CORE] == 0, other, own)


def check_sums(weights, value):
    column = jnp.sum(value * weights[...], axis=1, keepdims=True)
    return jnp.broadcast_to(column, (value.shape[0], LANES)).T[:ROWS, :]


def in_row(value, row):
    return jnp.where(lax.broadcasted_iota(jnp.int32, value.shape, 0) == row, value, 0.0)


def middle_kernel(place, ids, tile, *refs):
    starts, rights, outs, (held, sems) = refs[:2], refs[2:4], refs[4:6], refs[6:]
    k = ids[place]
    fetch([right.at[jnp.maximum(k, 0)] for right in rights], held, sems)

    @pl.when(k >= 0)
    def _():
        value = second(tile[...], 0)
        for s, (out, start) in enumerate(zip(outs, starts)):
            out[...] = start[...] + dot(held[s], value)

    @pl.when(k < 0)
    def _():
        for out, start in zip(outs, starts):
            out[...] = start[...]


def last_kernel(count, place, is_kept, arrive, ids, start, weights, *refs):
    if is_kept:
        square, blocks, *refs = refs
    right, *refs = refs
    if not is_kept:
        theirs, *refs = refs
    sources, out, held, held_sems, tiles, sems, *refs = refs[:count], *refs[count:]
    half, height = start.shape

    def copies(t):
        k = jnp.maximum(ids[place + t], 0)
        yield pltpu.make_async_copy(right.at[k], held.at[t], held_sems.at[t])
        yield pltpu.make_async_copy(sources[t], tiles.at[t], sems.at[t])

    if not is_kept:
        blocks, sem = refs
        blocks_copy = pltpu.make_async_copy(theirs.at[half:, :LANES], blocks, sem)
        blocks_copy.start()
    for t in range(count):

        @pl.when(ids[place + t] >= 0)
        def _():
            for copy in copies(t):
                copy.start()

    arrive()
    out[:half, :] = start[...]
    for t in range(count):

        @pl.when(ids[place + t] >= 0)
        def _():
            for copy in copies(t):
                copy.wait()
            out[:half, :] += dot(held[t], second(tiles[t], 0))

    out[half:, :] = jnp.zeros((ROWS, height), jnp.float32)
    out[half:, :half] = in_row(check_sums(weights, out[:half, :]), 1)
    if not is_kept:
        blocks_copy.wait()
    cube_term = spread(blocks[...], half, height) * out[:half, :]
    out[:half, :] = 3.0 * square[...] - 2.0 * cube_term if is_kept else -2.0 * cube_term


def diagonal_early_kernel(ids, *refs):
    lefts, out = refs[:-1], refs[-1]
    for j, left in enumerate(lefts):
        tile = left[: out.shape[0] // 2, :]
        term = dot(first(tile, 0), second(tile, 0), COLUMN_BY_COLUMN)
        out[...] = term if j == 0 else out[...] + term


def diagonal_kernel(ids, start, left, *refs):
    tiles, (given, kept, blocks, whole, held, sem) = refs[:-6], refs[-6:]
    half = given.shape[0]
    held[...] = jnp.zeros_like(held)
    for j, source in enumerate(tiles):

        @pl.when(ids[BACK] == j + 1)
        def _():
            copy = pltpu.make_async_copy(source.at[half:, :LANES], held, sem)
            copy.start()
            copy.wait()

    blocks[...] = held[...]
    tile = left[:half, :]
    whole[...] = start[...] + dot(first(tile, 0), second(tile, 0), COLUMN_BY_COLUMN)
    given[...] = whole[pl.ds(pl.multiple_of((1 - ids[CORE]) * half, half), half), :]
    kept[...] = whole[pl.ds(pl.multiple_of(ids[CORE] * half, half), half), :]


def early_kernel(ids, square, kept, received, blocks, kept_sum, received_sum, weights, *refs):
    rights, outs, (sums, held, sems) = refs[:2], refs[2:4], refs[4:]
    height = square.shape[1]
    fetch([right.at[place] for right in rights for place in (ids[COLUMN], ids[ROW])], held, sems)
    own = second(square[...], 0)
    diagonal = second((kept[...] + received[...]) * spread(blocks[...], *kept.shape), 0)
    for s, out in enumerate(outs):
        out[...] = dot(held[2 * s], own) + dot(held[2 * s + 1], diagonal)
    sums[...] = in_row(check_sums(weights, kept_sum[...] + received_sum[:, :height]), 0)


def in_steps(edges):
    sent, got, count = {}, {}, 0
    for source, target in edges:
        count = max(count, sum(e[0] == source for e in edges), sum(e[1] == target for e in edges))
    for source, target in edges:
        free = next(i for i in range(count) if (source, i) not in sent)
        other = next(i for i in range(count) if (target, i) not in got)
        if free != other:
            path, node, at_target, step = [], target, True, free
            while (node, step) in (got if at_target else sent):
                partner = (got if at_target else sent)[node, step]
                path.append((partner, node, step) if at_target else (node, partner, step))
                node, at_target, step = partner, not at_target, free + other - step
            for u, v, step in path:
                del sent[u, step], got[v, step]
            for u, v, step in path:
                sent[u, free + other - step], got[v, free + other - step] = v, u
        sent[source, free], got[target, free] = target, source
    return count, sent, got


def make_body(panels, columns):
    assert columns == 2 * panels and panels & (panels - 1) == 0
    chips = [(r, z) for r in range(panels) for z in range(panels)]

    edges = [((r, z), (z, z)) for r, z in chips if z != r]
    edges += [((r, z), (r, q)) for r, z in chips for q in range(panels) if z != r and q != r and q != z]
    steps, sent, got = in_steps(edges)
    down_step = [[-1] * panels for _ in range(panels)]
    tile_got = [[[-1] * steps for _ in range(panels)] for _ in range(panels)]
    for ((r, z), step), target in sent.items():
        if target[0] != r:
            down_step[r][z] = step
    for ((r, z), step), source in got.items():
        tile_got[r][z][step] = source[1] if source[0] == r else source[0]

    def send(value, target):
        pairs = []
        for r, z in chips:
            to = target(r, z)
            if to is not None:
                pairs += [(r * columns + 2 * z + core, to[0] * columns + 2 * to[1] + core) for core in (0, 1)]
        return lax.ppermute(value, ("row", "col"), pairs)

    def swap_core(value):
        return lax.ppermute(value, "col", [(c, c ^ 1) for c in range(columns)])

    def ring(step):
        return lambda r, z: (r, (z + step) % panels)

    def across(m):
        return lambda r, z: (r ^ m, z)

    def step_target(step, r, z):
        return sent.get(((r, z), step))

    powers = [1 << i for i in range(panels.bit_length() - 1)]

    def body(density, pattern, weights):
        r = lax.axis_index("row")
        c = lax.axis_index("col")
        z, core = c // 2, c % 2
        tile = density.T
        half, height = tile.shape

        scalars = [core, jnp.asarray(down_step)[r, z], r, z, (z - r) % panels]
        scalars += [r ^ m for m in range(panels)] + [(z - j) % panels for j in range(panels)]
        order = [1, 0, *range(2, steps)]
        scalars += [jnp.asarray(tile_got)[r, z, step] for step in order]
        ids = jnp.stack([jnp.asarray(s, jnp.int32) for s in scalars])
        line_at, steps_at = LISTS + panels, LISTS + 2 * panels

        packed, mine, other, blocks = call(
            pack_kernel,
            [shape(half + ROWS, height), shape(half, half), shape(half + ROWS, half), shape(ROWS, LANES)],
            jnp.asarray(core, jnp.int32)[None],
            tile,
            pattern.T,
        )
        left = {0: packed, 1: send(packed, ring(1))}
        theirs = swap_core(other)
        own = jnp.concatenate([mine, theirs[:half]], axis=1)
        tiles = {m: send(own, across(m)) for m in powers}
        own_later = after(own, *[tiles[m] for m in powers])
        tiles = [own] + [tiles[m] if m in powers else send(own_later, across(m)) for m in range(1, panels)]
        last = panels // 2 + 1
        for j in range(2, last):
            left[j] = send(left[j - 1], ring(1))
        for j in range(panels - 1, last - 1, -1):
            left[j] = send(after(packed, own) if j == panels - 1 else left[j + 1], ring(-1))

        part = shape(panels, half, 3 * half, dtype=jnp.bfloat16)
        kept, given = call(split_kernel, [part] * 2, ids, *tiles)

        early = [j for j in range(panels) if j != last]
        starts = call(
            functools.partial(early_products_kernel, early, line_at),
            [shape(half, height)] * 2,
            ids,
            *[left[j] for j in early],
            kept,
            given,
            placed=2,
            scratch=held_parts(2 * len(early), half),
            waits=True,
        )
        diagonal_start = call(diagonal_early_kernel, shape(height, height), ids, *[left[j] for j in early])
        kept_sum, given_sum = call(
            functools.partial(last_product_kernel, line_at + last),
            [shape(half, height), shape(half, height + half)],
            ids,
            left[last],
            after(starts[0], diagonal_start),
            starts[1],
            kept,
            given,
            placed=2,
            scratch=held_parts(2, half),
            waits=True,
        )
        diagonal_given, diagonal_kept, diagonal_blocks = call(
            diagonal_kernel,
            [shape(half, height)] * 2 + [shape(ROWS, LANES)],
            ids,
            diagonal_start,
            left[last],
            *[left[j] for j in range(1, panels)],
            placed=panels - 1,
            scratch=[
                pltpu.VMEM((height, height), jnp.float32),
                pltpu.VMEM((ROWS, LANES), jnp.float32),
                pltpu.SemaphoreType.DMA,
            ],
        )
        received = swap_core(given_sum)
        square, *rows = call(
            square_kernel,
            [shape(half, height)] * (1 + steps),
            ids,
            after(kept_sum, diagonal_given),
            given_sum,
            received,
            blocks,
            theirs,
            placed=1,
            scratch=[pltpu.VMEM((ROWS, LANES), jnp.float32), pltpu.SemaphoreType.DMA],
        )

        arrived = [send(rows[step], functools.partial(step_target, step)) for step in range(steps)]
        *cube, sums = call(
            early_kernel,
            [shape(half, height)] * 2 + [shape(ROWS, half)],
            ids,
            square,
            diagonal_kept,
            swap_core(diagonal_given),
            diagonal_blocks,
            kept_sum,
            received,
            weights[None, :],
            kept,
            given,
            placed=2,
            scratch=held_parts(4, half),
        )

        arrived = [arrived[step] for step in order]
        cube = call(
            functools.partial(middle_kernel, steps_at),
            [shape(half, height)] * 2,
            ids,
            arrived[0],
            *cube,
            kept,
            given,
            placed=2,
            scratch=held_parts(2, half),
        )
        steps_at, steps_left, arrived = steps_at + 1, steps - 1, arrived[1:]
        held = [pltpu.VMEM((steps_left, half, height), jnp.float32), pltpu.SemaphoreType.DMA((steps_left,))]

        kernel = functools.partial(last_kernel, steps_left, steps_at)
        out = shape(half + ROWS, height)
        scratch = held_parts(steps_left, half) + held
        given_cube = call(
            functools.partial(kernel, False),
            out,
            ids,
            cube[1],
            weights[None, :],
            given,
            theirs,
            *arrived,
            placed=steps_left + 2,
            waits=True,
            scratch=scratch + [pltpu.VMEM((ROWS, LANES), jnp.float32), pltpu.SemaphoreType.DMA],
        )
        kept_cube = call(
            functools.partial(kernel, True),
            out,
            ids,
            cube[0],
            weights[None, :],
            square,
            blocks,
            kept,
            *arrived,
            placed=steps_left + 1,
            waits=True,
            scratch=scratch,
        )
        received = swap_core(given_cube)
        sums = sums + kept_cube[half:, :half] + received[half:, :half]
        sums = sums + sum(send(sums, across(m)) for m in range(1, panels))
        return (kept_cube[:half] + received[:half]).T, sums[:2]

    return body


def solution(mesh):
    in_specs = (P("row", "col"), P("row", "col"), P("row"))
    out_specs = (P("row", "col"), P(None, "col"))
    body = make_body(mesh.shape["row"], mesh.shape["col"])
    return jax.shard_map(body, mesh=mesh, in_specs=in_specs, out_specs=out_specs, check_vma=False)
```
